32 devices in a mesh: ia: 4 (over y, x), ja: 8 (over z, core).
Axes of the slice: x: 2, y: 2, z: 4, core: 2. Of those that a mesh axis runs over, the one named last changes fastest.
Arguments:
- phase_space: float32 [12, 8192], P(None, 'ja'), may hold values from -6 to 6
- star_mass: float32 [8192], P('ja'), may hold values from 6.1035156e-05 to 0.00024414062
- star_level: int32 [8192], P('ja'), may hold values from 0 to 3
- active_ids: int32 [2, 64, 128], P(None, 'ia'), may hold values from 0 to 8191, as said below
- active_counts: int32 [2, 64], P(None, 'ia'), may hold values from 1 to 128, as said below
Outputs:
- final_state: float32 [12, 8192], P(None, 'ja')
- active_force: float32 [2, 6, 8192], P(None, None, ('ia', 'ja'))
The draws below stay inside these ranges and needn't reach their ends.
Inputs may be any that keep to these rules, and one draw needn't show every extreme that they name: `active_ids`: within one block step the 64 x 128 entries are distinct star numbers; entries of unused slots are ignored. `active_counts`: in every block step one block is full and one holds a single star.
All inputs are finite; a program needn't handle non-finite values.
Results may differ from the reference program's by a relative error of at most 0.00018.
Values sent between devices are 32-bit elements; how exact they have to be, the bound alone decides.
A program may use at most 64 MiB of HBM per device.

```python
import math
import jax
import jax.numpy as jnp
from jax import lax

ROW = 128
STEPS = 2
LEVELS = 4
STARS = 8192
BLOCKS = 64


def swap_into(order, slot, value):
    where_value = jnp.argmax((order == value).astype(jnp.int32)).astype(jnp.int32)
    held = order[slot]
    order = order.at[where_value].set(held)
    return order.at[slot].set(value)


def draw_active_ids(key, part):
    slots = BLOCKS * ROW
    stacked = []
    for step_index in range(STEPS):
        step_key = jax.random.fold_in(key, 11 + step_index)
        shuffled = jax.random.permutation(jax.random.fold_in(step_key, 1), STARS).astype(jnp.int32)
        marker = jax.random.randint(jax.random.fold_in(step_key, 2), (), 0, slots).astype(jnp.int32)
        second = ((marker + 1 + jax.random.randint(jax.random.fold_in(step_key, 3), (), 0, slots - 1)) % slots).astype(jnp.int32)
        shuffled = swap_into(shuffled, marker, STARS - 1)
        shuffled = swap_into(shuffled, second, 0)
        chosen = shuffled[:slots]
        stacked.append(chosen.reshape(BLOCKS, ROW))
    return jnp.stack(stacked).astype(jnp.int32)


def draw_active_counts(key, part):
    stacked = []
    for step_index in range(STEPS):
        step_key = jax.random.fold_in(key, 31 + step_index)
        filled = jax.random.randint(jax.random.fold_in(step_key, 1), (BLOCKS,), 1, ROW + 1)
        full_block = jax.random.randint(jax.random.fold_in(step_key, 2), (), 0, BLOCKS)
        single_block = (full_block + 1 + jax.random.randint(jax.random.fold_in(step_key, 3), (), 0, BLOCKS - 1)) % BLOCKS
        block_pos = jnp.arange(BLOCKS)
        filled = jnp.where(block_pos == full_block, ROW, filled)
        filled = jnp.where(block_pos == single_block, 1, filled)
        stacked.append(filled)
    return jnp.stack(stacked).astype(jnp.int32)


def place_ends(values, key, smallest, high):
    place = [jax.random.randint(jax.random.fold_in(key, axis), (), 0, length) for axis, length in enumerate(values.shape)]
    main_axis = values.shape.index(max(values.shape))
    neighbour = place[:main_axis] + [(place[main_axis] + 1) % values.shape[main_axis]] + place[main_axis + 1:]
    return values.at[tuple(place)].set(smallest).at[tuple(neighbour)].set(high)


def shard_levels(stream_key, shape, cuts, smallest, largest):
    factor_of, own = 1.0, jax.random.fold_in(stream_key, 6)
    for position, shards_of in cuts:
        steps = jnp.exp(jax.random.uniform(jax.random.fold_in(own, position), (shards_of,), jnp.float32, smallest / len(cuts), largest / len(cuts)))
        factor_of = factor_of * jnp.repeat(steps, shape[position] // shards_of).reshape([-1 if axis == position else 1 for axis in range(len(shape))])
    return factor_of


def gaussian(key, shape, width, reach, cuts=(), dtype=jnp.bfloat16):
    entries = jax.random.normal(key, shape, jnp.float32) * width
    if len(cuts) > 0:
        entries = shard_levels(key, shape, cuts, -0.22, 0.18) * entries
    return jnp.clip(entries, min=-reach, max=reach).astype(dtype)


def setup_inputs(seed: int = 0) -> dict:
    arg_keys = jax.random.split(jax.random.key(seed), 6)
    phase_space = gaussian(arg_keys[0], (12, STARS), 1.0, 6.0, ((1, 8),), jnp.float32)
    star_mass = jnp.clip(jnp.exp(math.log(0.00024414062) - 1.3862944 * jax.random.uniform(arg_keys[1], (STARS,), jnp.float32) ** shard_levels(arg_keys[1], (STARS,), ((0, 8),), -0.2, 0.2)), 6.103515625e-05, 0.00024414062)
    star_level = place_ends(jax.random.randint(arg_keys[2], (STARS,), 0, LEVELS), jax.random.fold_in(arg_keys[2], 1), 0, LEVELS - 1).astype(jnp.int32)
    active_ids = draw_active_ids(jax.random.fold_in(arg_keys[5], 71), 0)
    active_counts = draw_active_counts(jax.random.fold_in(arg_keys[5], 71), 0)
    return {"phase_space": phase_space, "star_mass": star_mass, "star_level": star_level, "active_ids": active_ids, "active_counts": active_counts}


EPS2 = 0.01
STEP_TIME = 0.05

def predict(state, tau):
    tau_sq = tau * tau
    tau_cube = tau_sq * tau
    new_pos = state[0:3] + state[3:6] * tau + state[6:9] * (tau_sq * 0.5) + state[9:12] * (tau_cube / 6.0)
    new_vel = state[3:6] + state[6:9] * tau + state[9:12] * (tau_sq * 0.5)
    return (new_pos, new_vel)

def field_force(target_pos, target_vel, source_pos, source_vel, source_mass):
    offset = source_pos[:, None, :] - target_pos[:, :, None]
    rel_vel = source_vel[:, None, :] - target_vel[:, :, None]
    dist_sq = lax.optimization_barrier(jnp.sum(offset * offset, axis=0)) + EPS2
    inverse = lax.rsqrt(dist_sq)
    weight = source_mass[None, :] * inverse * inverse * inverse
    radial = 3.0 * lax.optimization_barrier(jnp.sum(offset * rel_vel, axis=0)) / dist_sq
    accel = lax.optimization_barrier(jnp.sum(weight[None] * offset, axis=2))
    jolt = lax.optimization_barrier(jnp.sum(weight[None] * (rel_vel - radial[None] * offset), axis=2))
    return jnp.concatenate([accel, jolt], axis=0)

def blocked_force(target_pos, target_vel, source_pos, source_vel, source_mass, block_rows):
    total_rows = target_pos.shape[1]
    block_count = total_rows // block_rows
    tiles = (target_pos.reshape(3, block_count, block_rows).transpose(1, 0, 2), target_vel.reshape(3, block_count, block_rows).transpose(1, 0, 2))

    def one_tile(pair_tile):
        return field_force(pair_tile[0], pair_tile[1], source_pos, source_vel, source_mass)
    result = lax.map(one_tile, tiles)
    return result.transpose(1, 0, 2).reshape(6, total_rows)

def correct(active_rows, accel, jolt, span):
    half_step = span * 0.5
    twelfth = span * span / 12.0
    old_pos = active_rows[0:3]
    old_vel = active_rows[3:6]
    old_acc = active_rows[6:9]
    old_jerk = active_rows[9:12]
    new_vel = old_vel + (old_acc + accel) * half_step + (old_jerk - jolt) * twelfth
    new_pos = old_pos + (old_vel + new_vel) * half_step + (old_acc - accel) * twelfth
    return jnp.concatenate([new_pos, new_vel, accel, jolt], axis=0)

def reference(phase_space, star_mass, star_level, active_ids, active_counts):
    state = phase_space
    last = -STEP_TIME * star_level.astype(jnp.float32)
    force_steps = []
    for step_index in range(STEPS):
        clock = STEP_TIME * (step_index + 1)
        indices = active_ids[step_index].reshape(-1).astype(jnp.int32)
        slot_pos = lax.broadcasted_iota(jnp.int32, (active_ids.shape[1], active_ids.shape[2]), 1)
        usable = (slot_pos < active_counts[step_index][:, None]).reshape(-1)
        fpos, fvel = predict(state, clock - last)
        active_rows = state[:, indices]
        span = clock - last[indices]
        tpos, tvel = predict(active_rows, span)
        forces = blocked_force(tpos, tvel, fpos, fvel, star_mass, 64)
        force_steps.append(jnp.where(usable[None, :], forces, jnp.zeros_like(forces)))
        corrected = correct(active_rows, forces[0:3], forces[3:6], span)
        write_ids = jnp.where(usable, indices, STARS).astype(jnp.int32)
        state = state.at[:, write_ids].set(corrected, mode='drop')
        last = last.at[write_ids].set(clock, mode='drop')
    return (state, jnp.stack(force_steps))
```

```python
import functools

import jax
import jax.numpy as jnp
from jax import lax
from jax.experimental import pallas as pl
from jax.experimental.pallas import tpu as pltpu
from jax.sharding import PartitionSpec as P

STEPS = 2


EPS2 = 0.01
STEP_TIME = 0.05


def predict(state, tau):
    tau_sq = tau * tau
    tau_cube = tau_sq * tau
    new_pos = (
        state[0:3] + state[3:6] * tau + state[6:9] * (tau_sq * 0.5) + state[9:12] * (tau_cube / 6.0)
    )
    new_vel = state[3:6] + state[6:9] * tau + state[9:12] * (tau_sq * 0.5)
    return (new_pos, new_vel)


def field_force(target_pos, target_vel, source_pos, source_vel, source_mass):
    offset = source_pos[:, None, :] - target_pos[:, :, None]
    rel_vel = source_vel[:, None, :] - target_vel[:, :, None]
    dist_sq = jnp.sum(offset * offset, axis=0) + EPS2
    inverse = lax.rsqrt(dist_sq)
    weight = source_mass[None, :] * inverse * inverse * inverse
    radial = 3.0 * jnp.sum(offset * rel_vel, axis=0) / dist_sq
    accel = jnp.sum(weight[None] * offset, axis=2)
    jolt = jnp.sum(weight[None] * (rel_vel - radial[None] * offset), axis=2)
    return jnp.concatenate([accel, jolt], axis=0)


def blocked_force(target_pos, target_vel, source_pos, source_vel, source_mass, block_rows):
    total_rows = target_pos.shape[1]
    block_count = total_rows // block_rows
    tiles = (
        target_pos.reshape(3, block_count, block_rows).transpose(1, 0, 2),
        target_vel.reshape(3, block_count, block_rows).transpose(1, 0, 2),
    )

    def one_tile(pair_tile):
        return field_force(pair_tile[0], pair_tile[1], source_pos, source_vel, source_mass)

    result = lax.map(one_tile, tiles)
    return result.transpose(1, 0, 2).reshape(6, total_rows)


def correct(active_rows, accel, jolt, span):
    half_step = span * 0.5
    twelfth = span * span / 12.0
    old_pos = active_rows[0:3]
    old_vel = active_rows[3:6]
    old_acc = active_rows[6:9]
    old_jerk = active_rows[9:12]
    new_vel = old_vel + (old_acc + accel) * half_step + (old_jerk - jolt) * twelfth
    new_pos = old_pos + (old_vel + new_vel) * half_step + (old_acc - accel) * twelfth
    return jnp.concatenate([new_pos, new_vel, accel, jolt], axis=0)


def local(phase_space, star_mass, star_level, active_ids, active_counts):
    shard_width = phase_space.shape[1]
    shard_start = lax.axis_index("ja") * shard_width
    block_rows = 512
    state = phase_space
    last = -STEP_TIME * star_level.astype(jnp.float32)
    force_steps = []
    for step_index in range(STEPS):
        clock = STEP_TIME * (step_index + 1)
        indices = active_ids[step_index].reshape(-1)
        slot_pos = lax.broadcasted_iota(jnp.int32, (active_ids.shape[1], active_ids.shape[2]), 1)
        usable = (slot_pos < active_counts[step_index][:, None]).reshape(-1)
        local_ids = indices - shard_start
        inside = (local_ids >= 0) & (local_ids < shard_width)
        clipped = jnp.clip(local_ids, 0, shard_width - 1)
        fpos, fvel = predict(state, clock - last)
        stacked = jnp.concatenate([state, last[None, :]], axis=0)
        picked = jnp.where(inside[None, :], jnp.take(stacked, clipped, axis=1), 0.0)
        target_state = lax.psum(picked, "ja")
        tpos, tvel = predict(target_state[0:12], clock - target_state[12])
        partial_value = blocked_force(tpos, tvel, fpos, fvel, star_mass, block_rows)
        write_ids = jnp.where(usable, indices, -1)
        forces = lax.psum(partial_value, "ja")
        share_len = forces.shape[1] // lax.axis_size("ja")
        share_start = lax.axis_index("ja") * share_len
        force_share = lax.dynamic_slice_in_dim(forces, share_start, share_len, 1)
        usable_share = lax.dynamic_slice_in_dim(usable, share_start, share_len, 0)
        force_steps.append(jnp.where(usable_share[None, :], force_share, 0.0))
        outgoing = correct(target_state[0:12], forces[0:3], forces[3:6], clock - target_state[12])
        returned, return_ids = (
            lax.all_gather(outgoing, "ia", axis=1, tiled=True),
            lax.all_gather(write_ids, "ia", axis=0, tiled=True),
        )
        placed_raw = return_ids - shard_start
        valid = (return_ids >= 0) & (placed_raw >= 0) & (placed_raw < shard_width)
        placed = jnp.where(valid, placed_raw, shard_width)
        state = state.at[:, placed].set(returned, mode="drop")
        last = last.at[placed].set(clock, mode="drop")
    return (state, jnp.stack(force_steps))


MESH = pl.DeviceIdType.MESH
TILE = 16
VMEM = pl.BlockSpec(memory_space=pltpu.VMEM)


def pieces(values):
    high = values.astype(jnp.bfloat16)
    rest = values - high.astype(jnp.float32)
    middle = rest.astype(jnp.bfloat16)
    low = (rest - middle.astype(jnp.float32)).astype(jnp.bfloat16)
    return high, middle, low


def pick(values, onehot, dims):
    total = None
    for piece in pieces(values):
        term = lax.dot_general(piece, onehot, (dims, ((), ())), preferred_element_type=jnp.float32)
        total = term if total is None else total + term
    return total


def peers(sizes):
    num_i, num_j = sizes
    me_i, me_j = lax.axis_index("ia"), lax.axis_index("ja")
    along_j = [(me_i, lax.rem(me_j + step, num_j)) for step in range(1, num_j)]
    along_i = [(lax.rem(me_i + step, num_i), me_j) for step in range(1, num_i)]
    return along_j, along_i


def greet(others):
    barrier = pltpu.get_barrier_semaphore()
    for other in others:
        pl.semaphore_signal(barrier, inc=1, device_id=other, device_id_type=MESH)
    pl.semaphore_wait(barrier, len(others))


def send(source, target, send_sem, recv_sem, other):
    copy = pltpu.make_async_remote_copy(
        src_ref=source,
        dst_ref=target,
        send_sem=send_sem,
        recv_sem=recv_sem,
        device_id=other,
        device_id_type=MESH,
    )
    copy.start()
    return copy


def spread(sizes, all_ref, along_j, along_i, sj, rj, si, ri):
    me_i, me_j = lax.axis_index("ia"), lax.axis_index("ja")
    mine = all_ref.at[me_i, me_j]
    copies = [send(mine, mine, sj.at[n], rj.at[n], other) for n, other in enumerate(along_j)]
    for copy in copies:
        copy.wait()
    column = all_ref.at[me_i]
    return [send(column, column, si.at[n], ri.at[n], other) for n, other in enumerate(along_i)]


def first_kernel(sizes, state_ref, mass_ref, level_ref, ids_ref, all_ref, ids_all_ref, own_ref, sj, rj, si, ri, sk, rk):
    me_i, me_j = lax.axis_index("ia"), lax.axis_index("ja")
    width = own_ref.shape[1]
    part = pl.ds(pl.multiple_of(me_i * width, width), width)
    along_j, along_i = peers(sizes)
    greet(along_j + along_i)
    ids_all_ref[me_i] = ids_ref[...]
    named = ids_all_ref.at[me_i]
    copies = [send(named, named, sk.at[n], rk.at[n], other) for n, other in enumerate(along_i)]
    state = state_ref[:, part]
    mass = mass_ref[:, part]
    last = -STEP_TIME * level_ref[:, part].astype(jnp.float32)
    pos, vel = predict(state, STEP_TIME - last)
    all_ref[me_i, me_j, 0:3, :] = pos
    all_ref[me_i, me_j, 3:6, :] = vel
    all_ref[me_i, me_j, 6:8, :] = jnp.concatenate([mass, mass], axis=0)
    own_ref[0:12, :] = state
    own_ref[12:14, :] = jnp.concatenate([mass, last], axis=0)
    own_ref[14:24, :] = jnp.zeros((10, width), jnp.float32)
    copies += spread(sizes, all_ref, along_j, along_i, sj, rj, si, ri)
    for copy in copies:
        copy.wait()


def second_kernel(sizes, block_ref, all_ref, sj, rj, si, ri):
    me_i, me_j = lax.axis_index("ia"), lax.axis_index("ja")
    along_j, along_i = peers(sizes)
    greet(along_j + along_i)
    all_ref[me_i, me_j] = block_ref[...]
    for copy in spread(sizes, all_ref, along_j, along_i, sj, rj, si, ri):
        copy.wait()


def force_kernel(sizes, step_index, all_ref, ids_ref, own_ref, *refs):
    if step_index == 0:
        block_ref, new_ref, target_ref, total_ref = refs
    else:
        new_ref, target_ref, total_ref = refs
    num_i, num_j = sizes
    me_i, me_j = lax.axis_index("ia"), lax.axis_index("ja")
    width = own_ref.shape[1]
    lanes = 128
    clock = STEP_TIME * (step_index + 1)
    stars = (me_j * num_i + me_i) * width + lax.broadcasted_iota(jnp.int32, (width, lanes), 0)

    def match(row, seen):
        for inner in range(ids_ref.shape[3]):
            seen = jnp.where(ids_ref[row // num_j, step_index, lax.rem(row, num_j), inner : inner + 1, :] == stars, 1.0, seen)
        return seen

    seen = lax.fori_loop(0, num_i * num_j, match, jnp.zeros((width, lanes), jnp.float32))
    used_column = jnp.broadcast_to(jnp.max(seen, axis=1, keepdims=True), (width, lanes))
    used = jnp.transpose(used_column)[0:8]
    before = lax.broadcasted_iota(jnp.int32, (width, width), 0) < lax.broadcasted_iota(jnp.int32, (width, width), 1)
    before = jnp.where(before, 1.0, 0.0).astype(jnp.bfloat16)
    rank = jnp.dot(used.astype(jnp.bfloat16), before, preferred_element_type=jnp.float32)[0:1]
    used = used[0:1]
    wanted = jnp.where(used > 0.5, rank, -1.0).astype(jnp.int32)
    onehot = jnp.where(lax.broadcasted_iota(jnp.int32, (width, width), 0) == wanted, 1.0, 0.0).astype(jnp.bfloat16)
    count = jnp.sum(used).astype(jnp.int32)
    targets = None
    for piece in pieces(all_ref[me_i * num_j + me_j]):
        term = lax.dot_general(onehot, piece, (((1,), (1,)), ((), ())), preferred_element_type=jnp.float32)
        targets = term if targets is None else targets + term
    for row in range(6):
        target_ref[row] = jnp.broadcast_to(targets[:, row : row + 1], (width, lanes))
    total_ref[...] = jnp.zeros_like(total_ref)

    def tile(index, carry):
        rows = pl.ds(pl.multiple_of(index * TILE, TILE), TILE)
        tx, ty, tz, tu, tv, tw = [target_ref[row, rows, :] for row in range(6)]

        def chunk(block, sums):
            for first in range(0, width, lanes):
                sx, sy, sz, su, sv, sw, mass = [
                    all_ref[block, row : row + 1, first : first + lanes] for row in range(7)
                ]
                ax, ay, az, jx, jy, jz = sums
                dx, dy, dz = sx - tx, sy - ty, sz - tz
                wx, wy, wz = su - tu, sv - tv, sw - tw
                inverse = lax.rsqrt((dx * dx + dy * dy + dz * dz) + EPS2)
                square = inverse * inverse
                weight = (mass * inverse) * square
                radial = (dx * wx + dy * wy + dz * wz) * (3.0 * square)
                sums = (
                    ax + weight * dx,
                    ay + weight * dy,
                    az + weight * dz,
                    jx + weight * (wx - radial * dx),
                    jy + weight * (wy - radial * dy),
                    jz + weight * (wz - radial * dz),
                )
            return sums

        zero = jnp.zeros((TILE, lanes), jnp.float32)
        sums = lax.fori_loop(0, num_i * num_j, chunk, (zero,) * 6)
        for row in range(6):
            total_ref[row, rows, :] = sums[row]
        return carry

    lax.fori_loop(0, (count + TILE - 1) // TILE, tile, 0)
    lane = lax.broadcasted_iota(jnp.int32, (width, lanes), 1)
    packed = jnp.zeros((width, lanes), jnp.float32)
    for row in range(6):
        packed = jnp.where(lane == row, jnp.sum(total_ref[row], axis=1, keepdims=True), packed)
    force = pick(jnp.transpose(packed)[0:8], onehot, ((1,), (0,)))[0:6]
    state = own_ref[0:12, :]
    mass, last = own_ref[12:13, :], own_ref[13:14, :]
    moved = correct(state, force[0:3], force[3:6], clock - last)
    state = jnp.where(used > 0.5, moved, state)
    new_ref[0:12, :] = state
    if step_index == 0:
        last = jnp.where(used > 0.5, clock, last)
        new_ref[12:14, :] = jnp.concatenate([mass, last], axis=0)
        new_ref[14:18, :] = jnp.zeros((4, width), jnp.float32)
        new_ref[18:24, :] = force
        pos, vel = predict(state, STEP_TIME * (step_index + 2) - last)
        block_ref[0:3, :] = pos
        block_ref[3:6, :] = vel
        block_ref[6:8, :] = jnp.concatenate([mass, mass], axis=0)
    else:
        new_ref[12:18, :] = own_ref[18:24, :]
        new_ref[18:24, :] = force


def last_kernel(sizes, own_ref, ids_ref, state_ref, force_ref, rows_ref, part_ref, got_ref, si, ri, sj, rj):
    num_i, num_j = sizes
    me_i, me_j = lax.axis_index("ia"), lax.axis_index("ja")
    width = own_ref.shape[1]
    lanes = 128
    along_j, along_i = peers(sizes)
    greet(along_j + along_i)
    rows_ref[me_i] = own_ref[...]
    mine = rows_ref.at[me_i]
    copies = [send(mine, mine, si.at[n], ri.at[n], other) for n, other in enumerate(along_i)]
    for copy in copies:
        copy.wait()
    for block in range(num_i):
        state_ref[:, block * width : (block + 1) * width] = rows_ref[block, 0:12, :]
    star = me_j * (num_i * width) + lax.broadcasted_iota(jnp.int32, (num_i * width, lanes), 0)
    tables = []
    for step_index in range(STEPS):
        table = jnp.concatenate(
            [rows_ref[block, 12 + 6 * step_index : 18 + 6 * step_index, :] for block in range(num_i)], axis=1
        )
        table = jnp.concatenate([table, jnp.zeros((2, num_i * width), jnp.float32)], axis=0)
        tables.append(pieces(table))

    def share(owner, carry):
        for step_index in range(STEPS):
            for row in range(ids_ref.shape[2]):
                names = ids_ref[step_index, owner, row : row + 1, :]
                onehot = jnp.where(star == names, 1.0, 0.0).astype(jnp.bfloat16)
                total = None
                for piece in tables[step_index]:
                    term = jnp.dot(piece, onehot, preferred_element_type=jnp.float32)
                    total = term if total is None else total + term
                part_ref[owner, step_index, :, row * lanes : (row + 1) * lanes] = total
        return carry

    lax.fori_loop(0, num_j, share, 0)
    copies = [
        send(part_ref.at[other[1]], got_ref.at[me_j], sj.at[n], rj.at[n], other) for n, other in enumerate(along_j)
    ]
    for copy in copies:
        copy.wait()
    total = part_ref[me_j]
    for step in range(1, num_j):
        total = total + got_ref[lax.rem(me_j + step, num_j)]
    force_ref[...] = total[:, 0:6, :]


def star_order(sizes, phase_space, star_mass, star_level, active_ids, active_counts):
    num_i, num_j = sizes
    shard = phase_space.shape[1]
    width = shard // num_i
    f32 = jnp.float32
    rows, lanes = active_ids.shape[1], active_ids.shape[2]
    slot_pos = lax.broadcasted_iota(jnp.int32, active_ids.shape, 2)
    ids = jnp.where(slot_pos < active_counts[:, :, None], active_ids, -1)
    ids = ids.reshape(STEPS, num_j, rows // num_j, lanes)
    dma_j, dma_i = pltpu.SemaphoreType.DMA((num_j - 1,)), pltpu.SemaphoreType.DMA((num_i - 1,))
    whole = jax.ShapeDtypeStruct((num_i, num_j, 8, width), f32)
    own_shape = jax.ShapeDtypeStruct((24, width), f32)

    def remote(number):
        return pltpu.CompilerParams(collective_id=number, has_side_effects=True, vmem_limit_bytes=32 * 2**20)

    local_params = pltpu.CompilerParams(vmem_limit_bytes=32 * 2**20)
    every, ids_all, own = pl.pallas_call(
        functools.partial(first_kernel, sizes),
        out_shape=(whole, jax.ShapeDtypeStruct((num_i,) + ids.shape, jnp.int32), own_shape),
        in_specs=[VMEM] * 4,
        out_specs=(VMEM,) * 3,
        scratch_shapes=[dma_j, dma_j, dma_i, dma_i, dma_i, dma_i],
        compiler_params=remote(0),
    )(phase_space, star_mass.reshape(1, shard), star_level.reshape(1, shard), ids)
    work = [pltpu.VMEM((6, width, 128), f32), pltpu.VMEM((6, width, 128), f32)]
    block, own = pl.pallas_call(
        functools.partial(force_kernel, sizes, 0),
        out_shape=(jax.ShapeDtypeStruct((8, width), f32), own_shape),
        in_specs=[VMEM] * 3,
        out_specs=(VMEM,) * 2,
        scratch_shapes=work,
        compiler_params=local_params,
    )(every.reshape(num_i * num_j, 8, width), ids_all, own)
    every = pl.pallas_call(
        functools.partial(second_kernel, sizes),
        out_shape=whole,
        in_specs=[VMEM],
        out_specs=VMEM,
        scratch_shapes=[dma_j, dma_j, dma_i, dma_i],
        compiler_params=remote(1),
    )(block)
    own = pl.pallas_call(
        functools.partial(force_kernel, sizes, 1),
        out_shape=own_shape,
        in_specs=[VMEM] * 3,
        out_specs=VMEM,
        scratch_shapes=work,
        compiler_params=local_params,
    )(every.reshape(num_i * num_j, 8, width), ids_all, own)
    share = (rows // num_j) * lanes
    parts = pltpu.VMEM((num_j, STEPS, 8, share), f32)
    return pl.pallas_call(
        functools.partial(last_kernel, sizes),
        out_shape=(
            jax.ShapeDtypeStruct((12, shard), f32),
            jax.ShapeDtypeStruct((STEPS, 6, share), f32),
        ),
        in_specs=[VMEM] * 2,
        out_specs=(VMEM,) * 2,
        scratch_shapes=[pltpu.VMEM((num_i, 24, width), f32), parts, parts, dma_i, dma_i, dma_j, dma_j],
        compiler_params=remote(2),
    )(own, ids)


def solution(mesh):
    sizes = (mesh.shape["ia"], mesh.shape["ja"])
    placed = (P(None, "ja"), P("ja"), P("ja"), P(None, "ia", None), P(None, "ia"))

    def chosen(phase_space, star_mass, star_level, active_ids, active_counts):
        stars = phase_space.shape[1] * sizes[1]
        slots = active_ids.shape[1] * active_ids.shape[2] * sizes[0]
        if stars == slots:
            return star_order(sizes, phase_space, star_mass, star_level, active_ids, active_counts)
        return local(phase_space, star_mass, star_level, active_ids, active_counts)

    return jax.shard_map(
        chosen,
        mesh=mesh,
        in_specs=placed,
        out_specs=(P(None, "ja"), P(None, None, ("ia", "ja"))),
        check_vma=False,
    )
```

```python
import functools

import jax
import jax.numpy as jnp
from jax import lax
from jax.experimental import pallas as pl
from jax.experimental.pallas import tpu as pltpu
from jax.sharding import PartitionSpec as P

STEPS = 2


EPS2 = 0.01
STEP_TIME = 0.05


def predict(state, tau):
    tau_sq = tau * tau
    tau_cube = tau_sq * tau
    new_pos = (
        state[0:3] + state[3:6] * tau + state[6:9] * (tau_sq * 0.5) + state[9:12] * (tau_cube / 6.0)
    )
    new_vel = state[3:6] + state[6:9] * tau + state[9:12] * (tau_sq * 0.5)
    return (new_pos, new_vel)


def field_force(target_pos, target_vel, source_pos, source_vel, source_mass):
    offset = source_pos[:, None, :] - target_pos[:, :, None]
    rel_vel = source_vel[:, None, :] - target_vel[:, :, None]
    dist_sq = jnp.sum(offset * offset, axis=0) + EPS2
    inverse = lax.rsqrt(dist_sq)
    weight = source_mass[None, :] * inverse * inverse * inverse
    radial = 3.0 * jnp.sum(offset * rel_vel, axis=0) / dist_sq
    accel = jnp.sum(weight[None] * offset, axis=2)
    jolt = jnp.sum(weight[None] * (rel_vel - radial[None] * offset), axis=2)
    return jnp.concatenate([accel, jolt], axis=0)


def blocked_force(target_pos, target_vel, source_pos, source_vel, source_mass, block_rows):
    total_rows = target_pos.shape[1]
    block_count = total_rows // block_rows
    tiles = (
        target_pos.reshape(3, block_count, block_rows).transpose(1, 0, 2),
        target_vel.reshape(3, block_count, block_rows).transpose(1, 0, 2),
    )

    def one_tile(pair_tile):
        return field_force(pair_tile[0], pair_tile[1], source_pos, source_vel, source_mass)

    result = lax.map(one_tile, tiles)
    return result.transpose(1, 0, 2).reshape(6, total_rows)


def correct(active_rows, accel, jolt, span):
    half_step = span * 0.5
    twelfth = span * span / 12.0
    old_pos = active_rows[0:3]
    old_vel = active_rows[3:6]
    old_acc = active_rows[6:9]
    old_jerk = active_rows[9:12]
    new_vel = old_vel + (old_acc + accel) * half_step + (old_jerk - jolt) * twelfth
    new_pos = old_pos + (old_vel + new_vel) * half_step + (old_acc - accel) * twelfth
    return jnp.concatenate([new_pos, new_vel, accel, jolt], axis=0)


def local(phase_space, star_mass, star_level, active_ids, active_counts):
    shard_width = phase_space.shape[1]
    shard_start = lax.axis_index("ja") * shard_width
    block_rows = 512
    state = phase_space
    last = -STEP_TIME * star_level.astype(jnp.float32)
    force_steps = []
    for step_index in range(STEPS):
        clock = STEP_TIME * (step_index + 1)
        indices = active_ids[step_index].reshape(-1)
        slot_pos = lax.broadcasted_iota(jnp.int32, (active_ids.shape[1], active_ids.shape[2]), 1)
        usable = (slot_pos < active_counts[step_index][:, None]).reshape(-1)
        local_ids = indices - shard_start
        inside = (local_ids >= 0) & (local_ids < shard_width)
        clipped = jnp.clip(local_ids, 0, shard_width - 1)
        fpos, fvel = predict(state, clock - last)
        stacked = jnp.concatenate([state, last[None, :]], axis=0)
        picked = jnp.where(inside[None, :], jnp.take(stacked, clipped, axis=1), 0.0)
        target_state = lax.psum(picked, "ja")
        tpos, tvel = predict(target_state[0:12], clock - target_state[12])
        partial_value = blocked_force(tpos, tvel, fpos, fvel, star_mass, block_rows)
        write_ids = jnp.where(usable, indices, -1)
        forces = lax.psum(partial_value, "ja")
        share_len = forces.shape[1] // lax.axis_size("ja")
        share_start = lax.axis_index("ja") * share_len
        force_share = lax.dynamic_slice_in_dim(forces, share_start, share_len, 1)
        usable_share = lax.dynamic_slice_in_dim(usable, share_start, share_len, 0)
        force_steps.append(jnp.where(usable_share[None, :], force_share, 0.0))
        outgoing = correct(target_state[0:12], forces[0:3], forces[3:6], clock - target_state[12])
        returned, return_ids = (
            lax.all_gather(outgoing, "ia", axis=1, tiled=True),
            lax.all_gather(write_ids, "ia", axis=0, tiled=True),
        )
        placed_raw = return_ids - shard_start
        valid = (return_ids >= 0) & (placed_raw >= 0) & (placed_raw < shard_width)
        placed = jnp.where(valid, placed_raw, shard_width)
        state = state.at[:, placed].set(returned, mode="drop")
        last = last.at[placed].set(clock, mode="drop")
    return (state, jnp.stack(force_steps))


MESH = pl.DeviceIdType.MESH
TILE = 16
VMEM = pl.BlockSpec(memory_space=pltpu.VMEM)


def pieces(values):
    high = values.astype(jnp.bfloat16)
    rest = values - high.astype(jnp.float32)
    middle = rest.astype(jnp.bfloat16)
    low = (rest - middle.astype(jnp.float32)).astype(jnp.bfloat16)
    return high, middle, low


def peers(sizes):
    num_i, num_j = sizes
    me_i, me_j = lax.axis_index("ia"), lax.axis_index("ja")
    chips, chip, core = num_j // 2, me_j // 2, lax.rem(me_j, 2)
    steps = sorted(range(chips), key=lambda step: min(step, chips - step))
    along_j = []
    for step in steps:
        for flip in (0, 1):
            if step or flip:
                side = lax.rem(core + flip, 2)
                ahead = lax.rem(chip + step, chips) * 2 + side
                behind = lax.rem(chip + chips - step, chips) * 2 + side
                along_j.append(((me_i, ahead), behind))
    along_i = [((lax.rem(me_i + step, num_i), me_j), lax.rem(me_i + num_i - step, num_i)) for step in range(1, num_i)]
    return along_j, along_i


def send(source, target, send_sem, recv_sem, other):
    copy = pltpu.make_async_remote_copy(
        src_ref=source,
        dst_ref=target,
        send_sem=send_sem,
        recv_sem=recv_sem,
        device_id=other,
        device_id_type=MESH,
    )
    copy.start()
    return copy


def whole_kernel(
    sizes, state_ref, mass_ref, level_ref, ids_ref, out_ref, force_ref,
    ids_all, field, field_next, rows_a, rows_b, part, got, target_ref, total_ref,
    sk, rk, sf, rf, sg, rg, sa, ra, sb, rb, sp, rp, sq, rq,
):
    num_i, num_j = sizes
    me_i, me_j = lax.axis_index("ia"), lax.axis_index("ja")
    width, lanes = rows_a.shape[2], 128
    along_j, along_i = peers(sizes)
    own = pl.ds(pl.multiple_of(me_i * width, width), width)

    def to_column(named, ssem, rsem):
        return [send(named, named, ssem.at[n], rsem.at[n], other) for n, (other, _) in enumerate(along_i)]

    def to_row(named, ssem, rsem):
        return [send(named, named, ssem.at[n], rsem.at[n], other) for n, (other, _) in enumerate(along_j)]

    def used_row(step_index):
        stars = (me_j * num_i + me_i) * width + lax.broadcasted_iota(jnp.int32, (width, lanes), 0)

        def match(row, seen):
            for inner in range(ids_ref.shape[2]):
                names = ids_all[row // num_j, step_index, lax.rem(row, num_j), inner : inner + 1, :]
                seen = jnp.where(names == stars, 1.0, seen)
            return seen

        seen = lax.fori_loop(0, num_i * num_j, match, jnp.zeros((width, lanes), jnp.float32))
        column = jnp.broadcast_to(jnp.max(seen, axis=1, keepdims=True), (width, lanes))
        return jnp.transpose(column)[0:1] > 0.5

    def set_targets(rows):
        rows = jnp.concatenate([rows, jnp.zeros((lanes - 8, width), jnp.float32)], axis=0)
        columns = jnp.transpose(rows)
        for row in range(6):
            target_ref[row] = jnp.broadcast_to(columns[:, row : row + 1], (width, lanes))
        total_ref[...] = jnp.zeros_like(total_ref)

    def accumulate(source, owner):
        def tile(index, carry):
            rows = pl.ds(pl.multiple_of(index * TILE, TILE), TILE)
            tx, ty, tz, tu, tv, tw = [target_ref[row, rows, :] for row in range(6)]

            def chunk(block, sums):
                for first in range(0, width, lanes):
                    sx, sy, sz, su, sv, sw, mass = [
                        source[owner, block, row : row + 1, first : first + lanes] for row in range(7)
                    ]
                    ax, ay, az, jx, jy, jz = sums
                    dx, dy, dz = sx - tx, sy - ty, sz - tz
                    wx, wy, wz = su - tu, sv - tv, sw - tw
                    inverse = lax.rsqrt((dx * dx + dy * dy + dz * dz) + EPS2)
                    square = inverse * inverse
                    weight = (mass * inverse) * square
                    radial = (dx * wx + dy * wy + dz * wz) * (3.0 * square)
                    sums = (
                        ax + weight * dx,
                        ay + weight * dy,
                        az + weight * dz,
                        jx + weight * (wx - radial * dx),
                        jy + weight * (wy - radial * dy),
                        jz + weight * (wz - radial * dz),
                    )
                return sums

            sums = lax.fori_loop(0, num_i, chunk, tuple(total_ref[row, rows, :] for row in range(6)))
            for row in range(6):
                total_ref[row, rows, :] = sums[row]
            return carry

        lax.fori_loop(0, width // TILE, tile, 0)

    def totals():
        lane = lax.broadcasted_iota(jnp.int32, (width, lanes), 1)
        packed = jnp.zeros((width, lanes), jnp.float32)
        for row in range(6):
            packed = jnp.where(lane == row, jnp.sum(total_ref[row], axis=1, keepdims=True), packed)
        return jnp.transpose(packed)[0:6]

    def share(step_index, blocks):
        star = me_j * (num_i * width) + lax.broadcasted_iota(jnp.int32, (num_i * width, lanes), 0)
        table = pieces(jnp.concatenate(blocks, axis=1))
        tall = jnp.concatenate(table, axis=0)

        def fill(owner, carry):
            for row in range(ids_ref.shape[2]):
                names = ids_ref[step_index, owner, row : row + 1, :]
                onehot = jnp.where(star == names, 1.0, 0.0).astype(jnp.bfloat16)
                found = jnp.dot(tall, onehot, preferred_element_type=jnp.float32)
                part[step_index, owner, :, row * lanes : (row + 1) * lanes] = found[0:8] + found[8:16] + found[16:24]
            return carry

        lax.fori_loop(0, num_j, fill, 0)

    def send_parts(step_index, ssem, rsem):
        return [
            send(part.at[step_index, other[1]], got.at[step_index, me_j], ssem.at[n], rsem.at[n], other)
            for n, (other, _) in enumerate(along_j)
        ]

    greeting = [other for other, _ in along_j + along_i]
    barrier = pltpu.get_barrier_semaphore()
    for other in greeting:
        pl.semaphore_signal(barrier, inc=1, device_id=other, device_id_type=MESH)
    ids_all[me_i] = ids_ref[...]
    mass_all = mass_ref[...]
    pos, vel = predict(state_ref[...], STEP_TIME + STEP_TIME * level_ref[...].astype(jnp.float32))
    for block in range(num_i):
        some = slice(block * width, (block + 1) * width)
        field[me_j, block] = jnp.concatenate([pos[:, some], vel[:, some], mass_all[:, some], mass_all[:, some]], axis=0)
    pl.semaphore_wait(barrier, len(greeting))
    loose = to_column(ids_all.at[me_i], sk, rk)
    coming = to_row(field.at[me_j], sf, rf)
    set_targets(field[me_j, me_i])
    accumulate(field, me_j)
    for copy in loose:
        copy.wait()
    used = used_row(0)
    for copy, (_, owner) in zip(coming, along_j):
        copy.wait_recv()
        accumulate(field, owner)
    for copy in coming:
        copy.wait_send()
    force = totals()
    state = state_ref[:, own]
    last = -STEP_TIME * level_ref[:, own].astype(jnp.float32)
    state = jnp.where(used, correct(state, force[0:3], force[3:6], STEP_TIME - last), state)
    last = jnp.where(used, STEP_TIME, last)
    span = 2 * STEP_TIME - last
    pos, vel = predict(state, span)
    mass = mass_ref[:, own]
    field_next[me_j, me_i] = jnp.concatenate([pos, vel, mass, mass], axis=0)
    blank = jnp.zeros((2, width), jnp.float32)
    rows_a[me_i] = jnp.concatenate([force, blank], axis=0)
    column = to_column(field_next.at[me_j, me_i], sa, ra)
    column_force = to_column(rows_a.at[me_i], sp, rp)
    set_targets(field_next[me_j, me_i])
    used = used_row(1)
    for copy in column:
        copy.wait()
    coming = to_row(field_next.at[me_j], sg, rg)
    accumulate(field_next, me_j)
    for copy in column_force:
        copy.wait()
    share(0, [rows_a[block] for block in range(num_i)])
    for copy, (_, owner) in zip(coming, along_j):
        copy.wait_recv()
        accumulate(field_next, owner)
    for copy in coming:
        copy.wait_send()
    force = totals()
    state = jnp.where(used, correct(state, force[0:3], force[3:6], span), state)
    rows_b[me_i] = jnp.concatenate([force, blank[:, :], state, blank, blank], axis=0)
    column = to_column(rows_b.at[me_i], sb, rb)
    first_parts = send_parts(0, sq.at[0], rq.at[0])
    for copy in column:
        copy.wait()
    share(1, [rows_b[block, 0:8, :] for block in range(num_i)])
    second_parts = send_parts(1, sq.at[1], rq.at[1])
    for block in range(num_i):
        out_ref[:, block * width : (block + 1) * width] = rows_b[block, 8:20, :]
    for step_index, parts in enumerate((first_parts, second_parts)):
        for copy in parts:
            copy.wait()
        total = part[step_index, me_j]
        for _, owner in along_j:
            total = total + got[step_index, owner]
        force_ref[step_index] = total[0:6]


def star_order(sizes, phase_space, star_mass, star_level, active_ids, active_counts):
    num_i, num_j = sizes
    shard = phase_space.shape[1]
    width = shard // num_i
    f32 = jnp.float32
    rows, lanes = active_ids.shape[1], active_ids.shape[2]
    slot_pos = lax.broadcasted_iota(jnp.int32, active_ids.shape, 2)
    ids = jnp.where(slot_pos < active_counts[:, :, None], active_ids, -1)
    ids = ids.reshape(STEPS, num_j, rows // num_j, lanes)
    share = (rows // num_j) * lanes
    dma_j, dma_i = pltpu.SemaphoreType.DMA((num_j - 1,)), pltpu.SemaphoreType.DMA((num_i - 1,))
    dma_2 = pltpu.SemaphoreType.DMA((STEPS, num_j - 1))
    return pl.pallas_call(
        functools.partial(whole_kernel, sizes),
        out_shape=(jax.ShapeDtypeStruct((12, shard), f32), jax.ShapeDtypeStruct((STEPS, 6, share), f32)),
        in_specs=[VMEM] * 4,
        out_specs=(VMEM,) * 2,
        scratch_shapes=[
            pltpu.VMEM((num_i,) + ids.shape, jnp.int32),
            pltpu.VMEM((num_j, num_i, 8, width), f32),
            pltpu.VMEM((num_j, num_i, 8, width), f32),
            pltpu.VMEM((num_i, 8, width), f32),
            pltpu.VMEM((num_i, 24, width), f32),
            pltpu.VMEM((STEPS, num_j, 8, share), f32),
            pltpu.VMEM((STEPS, num_j, 8, share), f32),
            pltpu.VMEM((6, width, 128), f32),
            pltpu.VMEM((6, width, 128), f32),
            dma_i, dma_i, dma_j, dma_j, dma_j, dma_j, dma_i, dma_i, dma_i, dma_i, dma_i, dma_i, dma_2, dma_2,
        ],
        compiler_params=pltpu.CompilerParams(collective_id=0, has_side_effects=True, vmem_limit_bytes=32 * 2**20),
    )(phase_space, star_mass.reshape(1, shard), star_level.reshape(1, shard), ids)


def solution(mesh):
    sizes = (mesh.shape["ia"], mesh.shape["ja"])
    placed = (P(None, "ja"), P("ja"), P("ja"), P(None, "ia", None), P(None, "ia"))

    def chosen(phase_space, star_mass, star_level, active_ids, active_counts):
        stars = phase_space.shape[1] * sizes[1]
        slots = active_ids.shape[1] * active_ids.shape[2] * sizes[0]
        if stars == slots:
            return star_order(sizes, phase_space, star_mass, star_level, active_ids, active_counts)
        return local(phase_space, star_mass, star_level, active_ids, active_counts)

    return jax.shard_map(
        chosen,
        mesh=mesh,
        in_specs=placed,
        out_specs=(P(None, "ja"), P(None, None, ("ia", "ja"))),
        check_vma=False,
    )
```

```python
import functools

import jax
import jax.numpy as jnp
from jax import lax
from jax.experimental import pallas as pl
from jax.experimental.pallas import tpu as pltpu
from jax.sharding import PartitionSpec as P

STEPS = 2


EPS2 = 0.01
STEP_TIME = 0.05


def predict(state, tau):
    tau_sq = tau * tau
    tau_cube = tau_sq * tau
    new_pos = (
        state[0:3] + state[3:6] * tau + state[6:9] * (tau_sq * 0.5) + state[9:12] * (tau_cube / 6.0)
    )
    new_vel = state[3:6] + state[6:9] * tau + state[9:12] * (tau_sq * 0.5)
    return (new_pos, new_vel)


def field_force(target_pos, target_vel, source_pos, source_vel, source_mass):
    offset = source_pos[:, None, :] - target_pos[:, :, None]
    rel_vel = source_vel[:, None, :] - target_vel[:, :, None]
    dist_sq = jnp.sum(offset * offset, axis=0) + EPS2
    inverse = lax.rsqrt(dist_sq)
    weight = source_mass[None, :] * inverse * inverse * inverse
    radial = 3.0 * jnp.sum(offset * rel_vel, axis=0) / dist_sq
    accel = jnp.sum(weight[None] * offset, axis=2)
    jolt = jnp.sum(weight[None] * (rel_vel - radial[None] * offset), axis=2)
    return jnp.concatenate([accel, jolt], axis=0)


def blocked_force(target_pos, target_vel, source_pos, source_vel, source_mass, block_rows):
    total_rows = target_pos.shape[1]
    block_count = total_rows // block_rows
    tiles = (
        target_pos.reshape(3, block_count, block_rows).transpose(1, 0, 2),
        target_vel.reshape(3, block_count, block_rows).transpose(1, 0, 2),
    )

    def one_tile(pair_tile):
        return field_force(pair_tile[0], pair_tile[1], source_pos, source_vel, source_mass)

    result = lax.map(one_tile, tiles)
    return result.transpose(1, 0, 2).reshape(6, total_rows)


def correct(active_rows, accel, jolt, span):
    half_step = span * 0.5
    twelfth = span * span / 12.0
    old_pos = active_rows[0:3]
    old_vel = active_rows[3:6]
    old_acc = active_rows[6:9]
    old_jerk = active_rows[9:12]
    new_vel = old_vel + (old_acc + accel) * half_step + (old_jerk - jolt) * twelfth
    new_pos = old_pos + (old_vel + new_vel) * half_step + (old_acc - accel) * twelfth
    return jnp.concatenate([new_pos, new_vel, accel, jolt], axis=0)


def local(phase_space, star_mass, star_level, active_ids, active_counts):
    shard_width = phase_space.shape[1]
    shard_start = lax.axis_index("ja") * shard_width
    block_rows = 512
    state = phase_space
    last = -STEP_TIME * star_level.astype(jnp.float32)
    force_steps = []
    for step_index in range(STEPS):
        clock = STEP_TIME * (step_index + 1)
        indices = active_ids[step_index].reshape(-1)
        slot_pos = lax.broadcasted_iota(jnp.int32, (active_ids.shape[1], active_ids.shape[2]), 1)
        usable = (slot_pos < active_counts[step_index][:, None]).reshape(-1)
        local_ids = indices - shard_start
        inside = (local_ids >= 0) & (local_ids < shard_width)
        clipped = jnp.clip(local_ids, 0, shard_width - 1)
        fpos, fvel = predict(state, clock - last)
        stacked = jnp.concatenate([state, last[None, :]], axis=0)
        picked = jnp.where(inside[None, :], jnp.take(stacked, clipped, axis=1), 0.0)
        target_state = lax.psum(picked, "ja")
        tpos, tvel = predict(target_state[0:12], clock - target_state[12])
        partial_value = blocked_force(tpos, tvel, fpos, fvel, star_mass, block_rows)
        write_ids = jnp.where(usable, indices, -1)
        forces = lax.psum(partial_value, "ja")
        share_len = forces.shape[1] // lax.axis_size("ja")
        share_start = lax.axis_index("ja") * share_len
        force_share = lax.dynamic_slice_in_dim(forces, share_start, share_len, 1)
        usable_share = lax.dynamic_slice_in_dim(usable, share_start, share_len, 0)
        force_steps.append(jnp.where(usable_share[None, :], force_share, 0.0))
        outgoing = correct(target_state[0:12], forces[0:3], forces[3:6], clock - target_state[12])
        returned, return_ids = (
            lax.all_gather(outgoing, "ia", axis=1, tiled=True),
            lax.all_gather(write_ids, "ia", axis=0, tiled=True),
        )
        placed_raw = return_ids - shard_start
        valid = (return_ids >= 0) & (placed_raw >= 0) & (placed_raw < shard_width)
        placed = jnp.where(valid, placed_raw, shard_width)
        state = state.at[:, placed].set(returned, mode="drop")
        last = last.at[placed].set(clock, mode="drop")
    return (state, jnp.stack(force_steps))


MESH = pl.DeviceIdType.MESH
TILE = 16
VMEM = pl.BlockSpec(memory_space=pltpu.VMEM)


def pieces(values):
    high = values.astype(jnp.bfloat16)
    rest = values - high.astype(jnp.float32)
    middle = rest.astype(jnp.bfloat16)
    low = (rest - middle.astype(jnp.float32)).astype(jnp.bfloat16)
    return high, middle, low


def peers(sizes):
    num_i, num_j = sizes
    me_i, me_j = lax.axis_index("ia"), lax.axis_index("ja")
    chips, chip, core = num_j // 2, me_j // 2, lax.rem(me_j, 2)
    steps = sorted(range(chips), key=lambda step: min(step, chips - step))
    along_j = []
    for step in steps:
        for flip in (0, 1):
            if step or flip:
                side = lax.rem(core + flip, 2)
                ahead = lax.rem(chip + step, chips) * 2 + side
                behind = lax.rem(chip + chips - step, chips) * 2 + side
                along_j.append(((me_i, ahead), behind))
    along_i = [((lax.rem(me_i + step, num_i), me_j), lax.rem(me_i + num_i - step, num_i)) for step in range(1, num_i)]
    return along_j, along_i


def send(source, target, send_sem, recv_sem, other):
    copy = pltpu.make_async_remote_copy(
        src_ref=source,
        dst_ref=target,
        send_sem=send_sem,
        recv_sem=recv_sem,
        device_id=other,
        device_id_type=MESH,
    )
    copy.start()
    return copy


def whole_kernel(
    sizes, state_in, mass_ref, level_ref, raw_ref, counts_ref, out_ref, force_ref,
    state_ref, ids_all, field, field_next, rows_a, rows_b, part, got, target_ref, total_ref,
    load_sem, sk, rk, sf, rf, sg, rg, sa, ra, sb, rb, sp, rp, sq, rq,
):
    num_i, num_j = sizes
    me_i, me_j = lax.axis_index("ia"), lax.axis_index("ja")
    width, lanes = rows_a.shape[2], 128
    along_j, along_i = peers(sizes)
    own = pl.ds(pl.multiple_of(me_i * width, width), width)

    def to_column(named, ssem, rsem):
        return [send(named, named, ssem.at[n], rsem.at[n], other) for n, (other, _) in enumerate(along_i)]

    def to_row(named, ssem, rsem):
        return [send(named, named, ssem.at[n], rsem.at[n], other) for n, (other, _) in enumerate(along_j)]

    def used_row(step_index):
        stars = (me_j * num_i + me_i) * width + lax.broadcasted_iota(jnp.int32, (width, lanes), 0)

        def match(row, seen):
            for inner in range(ids_all.shape[3]):
                names = ids_all[row // num_j, step_index, lax.rem(row, num_j), inner : inner + 1, :]
                seen = jnp.where(names == stars, 1.0, seen)
            return seen

        seen = lax.fori_loop(0, num_i * num_j, match, jnp.zeros((width, lanes), jnp.float32))
        column = jnp.broadcast_to(jnp.max(seen, axis=1, keepdims=True), (width, lanes))
        return jnp.transpose(column)[0:1] > 0.5

    def set_targets(rows):
        rows = jnp.concatenate([rows, jnp.zeros((lanes - 8, width), jnp.float32)], axis=0)
        columns = jnp.transpose(rows)
        for row in range(6):
            target_ref[row] = jnp.broadcast_to(columns[:, row : row + 1], (width, lanes))
        total_ref[...] = jnp.zeros_like(total_ref)

    def accumulate(source, owner):
        def tile(index, carry):
            rows = pl.ds(pl.multiple_of(index * TILE, TILE), TILE)
            tx, ty, tz, tu, tv, tw = [target_ref[row, rows, :] for row in range(6)]

            def chunk(block, sums):
                for first in range(0, width, lanes):
                    sx, sy, sz, su, sv, sw, mass = [
                        source[owner, block, row : row + 1, first : first + lanes] for row in range(7)
                    ]
                    ax, ay, az, jx, jy, jz = sums
                    dx, dy, dz = sx - tx, sy - ty, sz - tz
                    wx, wy, wz = su - tu, sv - tv, sw - tw
                    inverse = lax.rsqrt((dx * dx + dy * dy + dz * dz) + EPS2)
                    square = inverse * inverse
                    weight = (mass * inverse) * square
                    radial = (dx * wx + dy * wy + dz * wz) * (3.0 * square)
                    sums = (
                        ax + weight * dx,
                        ay + weight * dy,
                        az + weight * dz,
                        jx + weight * (wx - radial * dx),
                        jy + weight * (wy - radial * dy),
                        jz + weight * (wz - radial * dz),
                    )
                return sums

            sums = lax.fori_loop(0, num_i, chunk, tuple(total_ref[row, rows, :] for row in range(6)), unroll=True)
            for row in range(6):
                total_ref[row, rows, :] = sums[row]
            return carry

        lax.fori_loop(0, width // TILE, tile, 0)

    def totals():
        lane = lax.broadcasted_iota(jnp.int32, (width, lanes), 1)
        packed = jnp.zeros((width, lanes), jnp.float32)
        for row in range(6):
            packed = jnp.where(lane == row, jnp.sum(total_ref[row], axis=1, keepdims=True), packed)
        return jnp.transpose(packed)[0:6]

    def share(step_index, blocks):
        star = me_j * (num_i * width) + lax.broadcasted_iota(jnp.int32, (num_i * width, lanes), 0)
        table = pieces(jnp.concatenate(blocks, axis=1))
        tall = jnp.concatenate(table, axis=0)

        def fill(owner, carry):
            for row in range(ids_all.shape[3]):
                names = ids_all[me_i, step_index, owner, row : row + 1, :]
                onehot = jnp.where(star == names, 1.0, 0.0).astype(jnp.bfloat16)
                found = jnp.dot(tall, onehot, preferred_element_type=jnp.float32)
                part[step_index, owner, :, row * lanes : (row + 1) * lanes] = found[0:8] + found[8:16] + found[16:24]
            return carry

        lax.fori_loop(0, num_j, fill, 0)

    def send_parts(step_index, ssem, rsem):
        return [
            send(part.at[step_index, other[1]], got.at[step_index, me_j], ssem.at[n], rsem.at[n], other)
            for n, (other, _) in enumerate(along_j)
        ]

    greeting = [other for other, _ in along_j + along_i]
    barrier = pltpu.get_barrier_semaphore()
    for other in greeting:
        pl.semaphore_signal(barrier, inc=1, device_id=other, device_id_type=MESH)
    load = pltpu.make_async_copy(state_in, state_ref, load_sem)
    load.start()
    per_owner = ids_all.shape[3]
    slot = lax.broadcasted_iota(jnp.int32, (1, lanes), 1)
    for step_index in range(STEPS):
        for row in range(raw_ref.shape[1]):
            names = jnp.where(slot < counts_ref[step_index, row], raw_ref[step_index, row : row + 1, :], -1)
            inner = row % per_owner
            ids_all[me_i, step_index, row // per_owner, inner : inner + 1, :] = names
    load.wait()
    mass_all = mass_ref[...]
    pos, vel = predict(state_ref[...], STEP_TIME + STEP_TIME * level_ref[...].astype(jnp.float32))
    for block in range(num_i):
        some = slice(block * width, (block + 1) * width)
        field[me_j, block] = jnp.concatenate([pos[:, some], vel[:, some], mass_all[:, some], mass_all[:, some]], axis=0)
    pl.semaphore_wait(barrier, len(greeting))
    loose = to_column(ids_all.at[me_i], sk, rk)
    coming = to_row(field.at[me_j], sf, rf)
    set_targets(field[me_j, me_i])
    accumulate(field, me_j)
    for copy in loose:
        copy.wait()
    used = used_row(0)
    for copy, (_, owner) in zip(coming, along_j):
        copy.wait_recv()
        accumulate(field, owner)
    for copy in coming:
        copy.wait_send()
    force = totals()
    state = state_ref[:, own]
    last = -STEP_TIME * level_ref[:, own].astype(jnp.float32)
    state = jnp.where(used, correct(state, force[0:3], force[3:6], STEP_TIME - last), state)
    last = jnp.where(used, STEP_TIME, last)
    span = 2 * STEP_TIME - last
    pos, vel = predict(state, span)
    mass = mass_ref[:, own]
    field_next[me_j, me_i] = jnp.concatenate([pos, vel, mass, mass], axis=0)
    blank = jnp.zeros((2, width), jnp.float32)
    rows_a[me_i] = jnp.concatenate([force, blank], axis=0)
    column = to_column(field_next.at[me_j, me_i], sa, ra)
    column_force = to_column(rows_a.at[me_i], sp, rp)
    set_targets(field_next[me_j, me_i])
    used = used_row(1)
    for copy in column:
        copy.wait()
    coming = to_row(field_next.at[me_j], sg, rg)
    accumulate(field_next, me_j)
    for copy in column_force:
        copy.wait()
    for copy, (_, owner) in zip(coming, along_j):
        copy.wait_recv()
        accumulate(field_next, owner)
    for copy in coming:
        copy.wait_send()
    force = totals()
    state = jnp.where(used, correct(state, force[0:3], force[3:6], span), state)
    rows_b[me_i] = jnp.concatenate([force, blank[:, :], state, blank, blank], axis=0)
    column = to_column(rows_b.at[me_i], sb, rb)
    share(0, [rows_a[block] for block in range(num_i)])
    first_parts = send_parts(0, sq.at[0], rq.at[0])
    for copy in column:
        copy.wait()
    share(1, [rows_b[block, 0:8, :] for block in range(num_i)])
    second_parts = send_parts(1, sq.at[1], rq.at[1])
    for block in range(num_i):
        out_ref[:, block * width : (block + 1) * width] = rows_b[block, 8:20, :]
    for step_index, parts in enumerate((first_parts, second_parts)):
        for copy in parts:
            copy.wait()
        total = part[step_index, me_j]
        for _, owner in along_j:
            total = total + got[step_index, owner]
        force_ref[step_index] = total[0:6]


def star_order(sizes, phase_space, star_mass, star_level, active_ids, active_counts):
    num_i, num_j = sizes
    shard = phase_space.shape[1]
    width = shard // num_i
    f32 = jnp.float32
    rows, lanes = active_ids.shape[1], active_ids.shape[2]
    share = (rows // num_j) * lanes
    dma_j, dma_i = pltpu.SemaphoreType.DMA((num_j - 1,)), pltpu.SemaphoreType.DMA((num_i - 1,))
    dma_2 = pltpu.SemaphoreType.DMA((STEPS, num_j - 1))
    return pl.pallas_call(
        functools.partial(whole_kernel, sizes),
        out_shape=(jax.ShapeDtypeStruct((12, shard), f32), jax.ShapeDtypeStruct((STEPS, 6, share), f32)),
        in_specs=[pl.BlockSpec(memory_space=pl.ANY), VMEM, VMEM, VMEM, pl.BlockSpec(memory_space=pltpu.SMEM)],
        out_specs=(VMEM,) * 2,
        scratch_shapes=[
            pltpu.VMEM((12, shard), f32),
            pltpu.VMEM((num_i, STEPS, num_j, rows // num_j, lanes), jnp.int32),
            pltpu.VMEM((num_j, num_i, 8, width), f32),
            pltpu.VMEM((num_j, num_i, 8, width), f32),
            pltpu.VMEM((num_i, 8, width), f32),
            pltpu.VMEM((num_i, 24, width), f32),
            pltpu.VMEM((STEPS, num_j, 8, share), f32),
            pltpu.VMEM((STEPS, num_j, 8, share), f32),
            pltpu.VMEM((6, width, 128), f32),
            pltpu.VMEM((6, width, 128), f32),
            pltpu.SemaphoreType.DMA, dma_i, dma_i, dma_j, dma_j, dma_j, dma_j, dma_i, dma_i, dma_i, dma_i, dma_i, dma_i, dma_2, dma_2,
        ],
        compiler_params=pltpu.CompilerParams(collective_id=0, has_side_effects=True, vmem_limit_bytes=32 * 2**20),
    )(phase_space, star_mass.reshape(1, shard), star_level.reshape(1, shard), active_ids, active_counts)


def solution(mesh):
    sizes = (mesh.shape["ia"], mesh.shape["ja"])
    placed = (P(None, "ja"), P("ja"), P("ja"), P(None, "ia", None), P(None, "ia"))

    def chosen(phase_space, star_mass, star_level, active_ids, active_counts):
        stars = phase_space.shape[1] * sizes[1]
        slots = active_ids.shape[1] * active_ids.shape[2] * sizes[0]
        if stars == slots:
            return star_order(sizes, phase_space, star_mass, star_level, active_ids, active_counts)
        return local(phase_space, star_mass, star_level, active_ids, active_counts)

    return jax.shard_map(
        chosen,
        mesh=mesh,
        in_specs=placed,
        out_specs=(P(None, "ja"), P(None, None, ("ia", "ja"))),
        check_vma=False,
    )
```

```python
import functools

import jax
import jax.numpy as jnp
from jax import lax
from jax.experimental import pallas as pl
from jax.experimental.pallas import tpu as pltpu
from jax.sharding import PartitionSpec as P

STEPS = 2


EPS2 = 0.01
STEP_TIME = 0.05


def predict(state, tau):
    tau_sq = tau * tau
    tau_cube = tau_sq * tau
    new_pos = (
        state[0:3] + state[3:6] * tau + state[6:9] * (tau_sq * 0.5) + state[9:12] * (tau_cube / 6.0)
    )
    new_vel = state[3:6] + state[6:9] * tau + state[9:12] * (tau_sq * 0.5)
    return (new_pos, new_vel)


def field_force(target_pos, target_vel, source_pos, source_vel, source_mass):
    offset = source_pos[:, None, :] - target_pos[:, :, None]
    rel_vel = source_vel[:, None, :] - target_vel[:, :, None]
    dist_sq = jnp.sum(offset * offset, axis=0) + EPS2
    inverse = lax.rsqrt(dist_sq)
    weight = source_mass[None, :] * inverse * inverse * inverse
    radial = 3.0 * jnp.sum(offset * rel_vel, axis=0) / dist_sq
    accel = jnp.sum(weight[None] * offset, axis=2)
    jolt = jnp.sum(weight[None] * (rel_vel - radial[None] * offset), axis=2)
    return jnp.concatenate([accel, jolt], axis=0)


def blocked_force(target_pos, target_vel, source_pos, source_vel, source_mass, block_rows):
    total_rows = target_pos.shape[1]
    block_count = total_rows // block_rows
    tiles = (
        target_pos.reshape(3, block_count, block_rows).transpose(1, 0, 2),
        target_vel.reshape(3, block_count, block_rows).transpose(1, 0, 2),
    )

    def one_tile(pair_tile):
        return field_force(pair_tile[0], pair_tile[1], source_pos, source_vel, source_mass)

    result = lax.map(one_tile, tiles)
    return result.transpose(1, 0, 2).reshape(6, total_rows)


def correct(active_rows, accel, jolt, span):
    half_step = span * 0.5
    twelfth = span * span / 12.0
    old_pos = active_rows[0:3]
    old_vel = active_rows[3:6]
    old_acc = active_rows[6:9]
    old_jerk = active_rows[9:12]
    new_vel = old_vel + (old_acc + accel) * half_step + (old_jerk - jolt) * twelfth
    new_pos = old_pos + (old_vel + new_vel) * half_step + (old_acc - accel) * twelfth
    return jnp.concatenate([new_pos, new_vel, accel, jolt], axis=0)


def local(phase_space, star_mass, star_level, active_ids, active_counts):
    shard_width = phase_space.shape[1]
    shard_start = lax.axis_index("ja") * shard_width
    block_rows = 512
    state = phase_space
    last = -STEP_TIME * star_level.astype(jnp.float32)
    force_steps = []
    for step_index in range(STEPS):
        clock = STEP_TIME * (step_index + 1)
        indices = active_ids[step_index].reshape(-1)
        slot_pos = lax.broadcasted_iota(jnp.int32, (active_ids.shape[1], active_ids.shape[2]), 1)
        usable = (slot_pos < active_counts[step_index][:, None]).reshape(-1)
        local_ids = indices - shard_start
        inside = (local_ids >= 0) & (local_ids < shard_width)
        clipped = jnp.clip(local_ids, 0, shard_width - 1)
        fpos, fvel = predict(state, clock - last)
        stacked = jnp.concatenate([state, last[None, :]], axis=0)
        picked = jnp.where(inside[None, :], jnp.take(stacked, clipped, axis=1), 0.0)
        target_state = lax.psum(picked, "ja")
        tpos, tvel = predict(target_state[0:12], clock - target_state[12])
        partial_value = blocked_force(tpos, tvel, fpos, fvel, star_mass, block_rows)
        write_ids = jnp.where(usable, indices, -1)
        forces = lax.psum(partial_value, "ja")
        share_len = forces.shape[1] // lax.axis_size("ja")
        share_start = lax.axis_index("ja") * share_len
        force_share = lax.dynamic_slice_in_dim(forces, share_start, share_len, 1)
        usable_share = lax.dynamic_slice_in_dim(usable, share_start, share_len, 0)
        force_steps.append(jnp.where(usable_share[None, :], force_share, 0.0))
        outgoing = correct(target_state[0:12], forces[0:3], forces[3:6], clock - target_state[12])
        returned, return_ids = (
            lax.all_gather(outgoing, "ia", axis=1, tiled=True),
            lax.all_gather(write_ids, "ia", axis=0, tiled=True),
        )
        placed_raw = return_ids - shard_start
        valid = (return_ids >= 0) & (placed_raw >= 0) & (placed_raw < shard_width)
        placed = jnp.where(valid, placed_raw, shard_width)
        state = state.at[:, placed].set(returned, mode="drop")
        last = last.at[placed].set(clock, mode="drop")
    return (state, jnp.stack(force_steps))


MESH = pl.DeviceIdType.MESH
TILE = 16
VMEM = pl.BlockSpec(memory_space=pltpu.VMEM)


def pieces(values):
    high = values.astype(jnp.bfloat16)
    rest = values - high.astype(jnp.float32)
    middle = rest.astype(jnp.bfloat16)
    low = (rest - middle.astype(jnp.float32)).astype(jnp.bfloat16)
    return high, middle, low


def peers(sizes):
    num_i, num_j = sizes
    me_i, me_j = lax.axis_index("ia"), lax.axis_index("ja")
    chips, chip, core = num_j // 2, me_j // 2, lax.rem(me_j, 2)
    steps = sorted(range(chips), key=lambda step: min(step, chips - step))
    along_j = []
    for step in steps:
        for flip in (0, 1):
            if step or flip:
                side = lax.rem(core + flip, 2)
                ahead = lax.rem(chip + step, chips) * 2 + side
                behind = lax.rem(chip + chips - step, chips) * 2 + side
                along_j.append(((me_i, ahead), behind))
    along_i = [((lax.rem(me_i + step, num_i), me_j), lax.rem(me_i + num_i - step, num_i)) for step in range(1, num_i)]
    return along_j, along_i


def send(source, target, send_sem, recv_sem, other):
    copy = pltpu.make_async_remote_copy(
        src_ref=source,
        dst_ref=target,
        send_sem=send_sem,
        recv_sem=recv_sem,
        device_id=other,
        device_id_type=MESH,
    )
    copy.start()
    return copy


def whole_kernel(
    sizes, state_in, mass_in, level_in, raw_in, counts_in, out_ref, force_ref,
    state_ref, mass_ref, level_ref, raw_ref, counts_ref, ids_all, field, field_next, rows_a, rows_b, part, got, target_ref, total_ref,
    load_sem, sk, rk, sf, rf, sg, rg, sa, ra, sb, rb, sp, rp, sq, rq,
):
    num_i, num_j = sizes
    me_i, me_j = lax.axis_index("ia"), lax.axis_index("ja")
    width, lanes = rows_a.shape[2], 128
    along_j, along_i = peers(sizes)
    own = pl.ds(pl.multiple_of(me_i * width, width), width)

    def to_column(named, ssem, rsem):
        return [send(named, named, ssem.at[n], rsem.at[n], other) for n, (other, _) in enumerate(along_i)]

    def to_row(named, ssem, rsem):
        return [send(named, named, ssem.at[n], rsem.at[n], other) for n, (other, _) in enumerate(along_j)]

    def used_row(step_index):
        stars = (me_j * num_i + me_i) * width + lax.broadcasted_iota(jnp.int32, (width, lanes), 0)

        def match(row, seen):
            for inner in range(ids_all.shape[3]):
                names = ids_all[row // num_j, step_index, lax.rem(row, num_j), inner : inner + 1, :]
                seen = jnp.where(names == stars, 1.0, seen)
            return seen

        seen = lax.fori_loop(0, num_i * num_j, match, jnp.zeros((width, lanes), jnp.float32))
        column = jnp.broadcast_to(jnp.max(seen, axis=1, keepdims=True), (width, lanes))
        return jnp.transpose(column)[0:1] > 0.5

    def set_targets(rows):
        rows = jnp.concatenate([rows, jnp.zeros((lanes - 8, width), jnp.float32)], axis=0)
        columns = jnp.transpose(rows)
        for row in range(6):
            target_ref[row] = jnp.broadcast_to(columns[:, row : row + 1], (width, lanes))
        total_ref[...] = jnp.zeros_like(total_ref)

    def accumulate(source, owner):
        def tile(index, carry):
            rows = pl.ds(pl.multiple_of(index * TILE, TILE), TILE)
            tx, ty, tz, tu, tv, tw = [target_ref[row, rows, :] for row in range(6)]

            def chunk(block, sums):
                for first in range(0, width, lanes):
                    sx, sy, sz, su, sv, sw, mass = [
                        source[owner, block, row : row + 1, first : first + lanes] for row in range(7)
                    ]
                    ax, ay, az, jx, jy, jz = sums
                    dx, dy, dz = sx - tx, sy - ty, sz - tz
                    wx, wy, wz = su - tu, sv - tv, sw - tw
                    inverse = lax.rsqrt((dx * dx + dy * dy + dz * dz) + EPS2)
                    square = inverse * inverse
                    weight = (mass * inverse) * square
                    radial = (dx * wx + dy * wy + dz * wz) * (3.0 * square)
                    sums = (
                        ax + weight * dx,
                        ay + weight * dy,
                        az + weight * dz,
                        jx + weight * (wx - radial * dx),
                        jy + weight * (wy - radial * dy),
                        jz + weight * (wz - radial * dz),
                    )
                return sums

            sums = lax.fori_loop(0, num_i, chunk, tuple(total_ref[row, rows, :] for row in range(6)), unroll=True)
            for row in range(6):
                total_ref[row, rows, :] = sums[row]
            return carry

        lax.fori_loop(0, width // TILE, tile, 0)

    def totals():
        lane = lax.broadcasted_iota(jnp.int32, (width, lanes), 1)
        packed = jnp.zeros((width, lanes), jnp.float32)
        for row in range(6):
            packed = jnp.where(lane == row, jnp.sum(total_ref[row], axis=1, keepdims=True), packed)
        return jnp.transpose(packed)[0:6]

    def share(step_index, blocks):
        star = me_j * (num_i * width) + lax.broadcasted_iota(jnp.int32, (num_i * width, lanes), 0)
        table = pieces(jnp.concatenate(blocks, axis=1))
        tall = jnp.concatenate(table, axis=0)

        def fill(owner, carry):
            for row in range(ids_all.shape[3]):
                names = ids_all[me_i, step_index, owner, row : row + 1, :]
                onehot = jnp.where(star == names, 1.0, 0.0).astype(jnp.bfloat16)
                found = jnp.dot(tall, onehot, preferred_element_type=jnp.float32)
                part[step_index, owner, :, row * lanes : (row + 1) * lanes] = found[0:8] + found[8:16] + found[16:24]
            return carry

        lax.fori_loop(0, num_j, fill, 0)

    def send_parts(step_index, ssem, rsem):
        return [
            send(part.at[step_index, other[1]], got.at[step_index, me_j], ssem.at[n], rsem.at[n], other)
            for n, (other, _) in enumerate(along_j)
        ]

    loads = [
        pltpu.make_async_copy(source, target, load_sem.at[n])
        for n, (source, target) in enumerate((
            (counts_in, counts_ref), (raw_in, raw_ref), (level_in, level_ref), (mass_in, mass_ref), (state_in, state_ref)
        ))
    ]
    for copy in loads:
        copy.start()
    greeting = [other for other, _ in along_j + along_i]
    barrier = pltpu.get_barrier_semaphore()
    for other in greeting:
        pl.semaphore_signal(barrier, inc=1, device_id=other, device_id_type=MESH)
    for copy in loads:
        copy.wait()
    per_owner = ids_all.shape[3]
    slot = lax.broadcasted_iota(jnp.int32, (1, lanes), 1)
    for step_index in range(STEPS):
        for row in range(raw_ref.shape[1]):
            names = jnp.where(slot < counts_ref[step_index, row], raw_ref[step_index, row : row + 1, :], -1)
            inner = row % per_owner
            ids_all[me_i, step_index, row // per_owner, inner : inner + 1, :] = names
    mass_all = mass_ref[...]
    pos, vel = predict(state_ref[...], STEP_TIME + STEP_TIME * level_ref[...].astype(jnp.float32))
    for block in range(num_i):
        some = slice(block * width, (block + 1) * width)
        field[me_j, block] = jnp.concatenate([pos[:, some], vel[:, some], mass_all[:, some], mass_all[:, some]], axis=0)
    pl.semaphore_wait(barrier, len(greeting))
    loose = to_column(ids_all.at[me_i], sk, rk)
    coming = to_row(field.at[me_j], sf, rf)
    set_targets(field[me_j, me_i])
    accumulate(field, me_j)
    for copy in loose:
        copy.wait()
    used = used_row(0)
    for copy, (_, owner) in zip(coming, along_j):
        copy.wait_recv()
        accumulate(field, owner)
    for copy in coming:
        copy.wait_send()
    force = totals()
    state = state_ref[:, own]
    last = -STEP_TIME * level_ref[:, own].astype(jnp.float32)
    state = jnp.where(used, correct(state, force[0:3], force[3:6], STEP_TIME - last), state)
    last = jnp.where(used, STEP_TIME, last)
    span = 2 * STEP_TIME - last
    pos, vel = predict(state, span)
    mass = mass_ref[:, own]
    field_next[me_j, me_i] = jnp.concatenate([pos, vel, mass, mass], axis=0)
    blank = jnp.zeros((2, width), jnp.float32)
    rows_a[me_i] = jnp.concatenate([force, blank], axis=0)
    column = to_column(field_next.at[me_j, me_i], sa, ra)
    column_force = to_column(rows_a.at[me_i], sp, rp)
    set_targets(field_next[me_j, me_i])
    used = used_row(1)
    for copy in column:
        copy.wait()
    coming = to_row(field_next.at[me_j], sg, rg)
    accumulate(field_next, me_j)
    for copy in column_force:
        copy.wait()
    for copy, (_, owner) in zip(coming, along_j):
        copy.wait_recv()
        accumulate(field_next, owner)
    for copy in coming:
        copy.wait_send()
    force = totals()
    state = jnp.where(used, correct(state, force[0:3], force[3:6], span), state)
    rows_b[me_i] = jnp.concatenate([force, blank[:, :], state, blank, blank], axis=0)
    column = to_column(rows_b.at[me_i], sb, rb)
    share(0, [rows_a[block] for block in range(num_i)])
    first_parts = send_parts(0, sq.at[0], rq.at[0])
    for copy in column:
        copy.wait()
    share(1, [rows_b[block, 0:8, :] for block in range(num_i)])
    second_parts = send_parts(1, sq.at[1], rq.at[1])
    for block in range(num_i):
        out_ref[:, block * width : (block + 1) * width] = rows_b[block, 8:20, :]
    for step_index, parts in enumerate((first_parts, second_parts)):
        for copy in parts:
            copy.wait()
        total = part[step_index, me_j]
        for _, owner in along_j:
            total = total + got[step_index, owner]
        force_ref[step_index] = total[0:6]


def star_order(sizes, phase_space, star_mass, star_level, active_ids, active_counts):
    num_i, num_j = sizes
    shard = phase_space.shape[1]
    width = shard // num_i
    f32 = jnp.float32
    rows, lanes = active_ids.shape[1], active_ids.shape[2]
    share = (rows // num_j) * lanes
    dma_j, dma_i = pltpu.SemaphoreType.DMA((num_j - 1,)), pltpu.SemaphoreType.DMA((num_i - 1,))
    dma_2 = pltpu.SemaphoreType.DMA((STEPS, num_j - 1))
    return pl.pallas_call(
        functools.partial(whole_kernel, sizes),
        out_shape=(jax.ShapeDtypeStruct((12, shard), f32), jax.ShapeDtypeStruct((STEPS, 6, share), f32)),
        in_specs=[pl.BlockSpec(memory_space=pltpu.HBM)] * 5,
        out_specs=(VMEM,) * 2,
        scratch_shapes=[
            pltpu.VMEM((12, shard), f32),
            pltpu.VMEM((1, shard), f32),
            pltpu.VMEM((1, shard), jnp.int32),
            pltpu.VMEM(active_ids.shape, jnp.int32),
            pltpu.SMEM(active_counts.shape, jnp.int32),
            pltpu.VMEM((num_i, STEPS, num_j, rows // num_j, lanes), jnp.int32),
            pltpu.VMEM((num_j, num_i, 8, width), f32),
            pltpu.VMEM((num_j, num_i, 8, width), f32),
            pltpu.VMEM((num_i, 8, width), f32),
            pltpu.VMEM((num_i, 24, width), f32),
            pltpu.VMEM((STEPS, num_j, 8, share), f32),
            pltpu.VMEM((STEPS, num_j, 8, share), f32),
            pltpu.VMEM((6, width, 128), f32),
            pltpu.VMEM((6, width, 128), f32),
            pltpu.SemaphoreType.DMA((5,)), dma_i, dma_i, dma_j, dma_j, dma_j, dma_j, dma_i, dma_i, dma_i, dma_i, dma_i, dma_i, dma_2, dma_2,
        ],
        compiler_params=pltpu.CompilerParams(collective_id=0, has_side_effects=True, vmem_limit_bytes=32 * 2**20),
    )(phase_space, star_mass.reshape(1, shard), star_level.reshape(1, shard), active_ids, active_counts)


def solution(mesh):
    sizes = (mesh.shape["ia"], mesh.shape["ja"])
    placed = (P(None, "ja"), P("ja"), P("ja"), P(None, "ia", None), P(None, "ia"))

    def chosen(phase_space, star_mass, star_level, active_ids, active_counts):
        stars = phase_space.shape[1] * sizes[1]
        slots = active_ids.shape[1] * active_ids.shape[2] * sizes[0]
        if stars == slots:
            return star_order(sizes, phase_space, star_mass, star_level, active_ids, active_counts)
        return local(phase_space, star_mass, star_level, active_ids, active_counts)

    return jax.shard_map(
        chosen,
        mesh=mesh,
        in_specs=placed,
        out_specs=(P(None, "ja"), P(None, None, ("ia", "ja"))),
        check_vma=False,
    )
```

```python
import functools

import jax
import jax.numpy as jnp
from jax import lax
from jax.experimental import pallas as pl
from jax.experimental.pallas import tpu as pltpu
from jax.sharding import PartitionSpec as P

STEPS = 2


EPS2 = 0.01
STEP_TIME = 0.05


def predict(state, tau):
    tau_sq = tau * tau
    tau_cube = tau_sq * tau
    new_pos = (
        state[0:3] + state[3:6] * tau + state[6:9] * (tau_sq * 0.5) + state[9:12] * (tau_cube / 6.0)
    )
    new_vel = state[3:6] + state[6:9] * tau + state[9:12] * (tau_sq * 0.5)
    return (new_pos, new_vel)


def field_force(target_pos, target_vel, source_pos, source_vel, source_mass):
    offset = source_pos[:, None, :] - target_pos[:, :, None]
    rel_vel = source_vel[:, None, :] - target_vel[:, :, None]
    dist_sq = jnp.sum(offset * offset, axis=0) + EPS2
    inverse = lax.rsqrt(dist_sq)
    weight = source_mass[None, :] * inverse * inverse * inverse
    radial = 3.0 * jnp.sum(offset * rel_vel, axis=0) / dist_sq
    accel = jnp.sum(weight[None] * offset, axis=2)
    jolt = jnp.sum(weight[None] * (rel_vel - radial[None] * offset), axis=2)
    return jnp.concatenate([accel, jolt], axis=0)


def blocked_force(target_pos, target_vel, source_pos, source_vel, source_mass, block_rows):
    total_rows = target_pos.shape[1]
    block_count = total_rows // block_rows
    tiles = (
        target_pos.reshape(3, block_count, block_rows).transpose(1, 0, 2),
        target_vel.reshape(3, block_count, block_rows).transpose(1, 0, 2),
    )

    def one_tile(pair_tile):
        return field_force(pair_tile[0], pair_tile[1], source_pos, source_vel, source_mass)

    result = lax.map(one_tile, tiles)
    return result.transpose(1, 0, 2).reshape(6, total_rows)


def correct(active_rows, accel, jolt, span):
    half_step = span * 0.5
    twelfth = span * span / 12.0
    old_pos = active_rows[0:3]
    old_vel = active_rows[3:6]
    old_acc = active_rows[6:9]
    old_jerk = active_rows[9:12]
    new_vel = old_vel + (old_acc + accel) * half_step + (old_jerk - jolt) * twelfth
    new_pos = old_pos + (old_vel + new_vel) * half_step + (old_acc - accel) * twelfth
    return jnp.concatenate([new_pos, new_vel, accel, jolt], axis=0)


def local(phase_space, star_mass, star_level, active_ids, active_counts):
    shard_width = phase_space.shape[1]
    shard_start = lax.axis_index("ja") * shard_width
    block_rows = 512
    state = phase_space
    last = -STEP_TIME * star_level.astype(jnp.float32)
    force_steps = []
    for step_index in range(STEPS):
        clock = STEP_TIME * (step_index + 1)
        indices = active_ids[step_index].reshape(-1)
        slot_pos = lax.broadcasted_iota(jnp.int32, (active_ids.shape[1], active_ids.shape[2]), 1)
        usable = (slot_pos < active_counts[step_index][:, None]).reshape(-1)
        local_ids = indices - shard_start
        inside = (local_ids >= 0) & (local_ids < shard_width)
        clipped = jnp.clip(local_ids, 0, shard_width - 1)
        fpos, fvel = predict(state, clock - last)
        stacked = jnp.concatenate([state, last[None, :]], axis=0)
        picked = jnp.where(inside[None, :], jnp.take(stacked, clipped, axis=1), 0.0)
        target_state = lax.psum(picked, "ja")
        tpos, tvel = predict(target_state[0:12], clock - target_state[12])
        partial_value = blocked_force(tpos, tvel, fpos, fvel, star_mass, block_rows)
        write_ids = jnp.where(usable, indices, -1)
        forces = lax.psum(partial_value, "ja")
        share_len = forces.shape[1] // lax.axis_size("ja")
        share_start = lax.axis_index("ja") * share_len
        force_share = lax.dynamic_slice_in_dim(forces, share_start, share_len, 1)
        usable_share = lax.dynamic_slice_in_dim(usable, share_start, share_len, 0)
        force_steps.append(jnp.where(usable_share[None, :], force_share, 0.0))
        outgoing = correct(target_state[0:12], forces[0:3], forces[3:6], clock - target_state[12])
        returned, return_ids = (
            lax.all_gather(outgoing, "ia", axis=1, tiled=True),
            lax.all_gather(write_ids, "ia", axis=0, tiled=True),
        )
        placed_raw = return_ids - shard_start
        valid = (return_ids >= 0) & (placed_raw >= 0) & (placed_raw < shard_width)
        placed = jnp.where(valid, placed_raw, shard_width)
        state = state.at[:, placed].set(returned, mode="drop")
        last = last.at[placed].set(clock, mode="drop")
    return (state, jnp.stack(force_steps))


MESH = pl.DeviceIdType.MESH
TILE = 16
VMEM = pl.BlockSpec(memory_space=pltpu.VMEM)


def pieces(values):
    high = values.astype(jnp.bfloat16)
    rest = values - high.astype(jnp.float32)
    middle = rest.astype(jnp.bfloat16)
    low = (rest - middle.astype(jnp.float32)).astype(jnp.bfloat16)
    return high, middle, low


def peers(sizes):
    num_i, num_j = sizes
    me_i, me_j = lax.axis_index("ia"), lax.axis_index("ja")
    chips, chip, core = num_j // 2, me_j // 2, lax.rem(me_j, 2)
    steps = sorted(range(chips), key=lambda step: min(step, chips - step))
    along_j = []
    for step in steps:
        for flip in (0, 1):
            if step or flip:
                side = lax.rem(core + flip, 2)
                ahead = lax.rem(chip + step, chips) * 2 + side
                behind = lax.rem(chip + chips - step, chips) * 2 + side
                along_j.append(((me_i, ahead), behind))
    along_i = [((lax.rem(me_i + step, num_i), me_j), lax.rem(me_i + num_i - step, num_i)) for step in range(1, num_i)]
    return along_j, along_i


def send(source, target, send_sem, recv_sem, other):
    copy = pltpu.make_async_remote_copy(
        src_ref=source,
        dst_ref=target,
        send_sem=send_sem,
        recv_sem=recv_sem,
        device_id=other,
        device_id_type=MESH,
    )
    copy.start()
    return copy


def whole_kernel(
    sizes, state_in, mass_in, level_in, raw_in, counts_in, out_ref, force_ref,
    state_ref, mass_ref, level_ref, raw_ref, counts_ref, ids_all, field, field_next, rows_a, rows_b, part, got, target_ref, total_ref,
    load_sem, sk, rk, sf, rf, sg, rg, sa, ra, sb, rb, sp, rp, sq, rq,
):
    num_i, num_j = sizes
    me_i, me_j = lax.axis_index("ia"), lax.axis_index("ja")
    width, lanes = rows_a.shape[2], 128
    along_j, along_i = peers(sizes)
    own = pl.ds(pl.multiple_of(me_i * width, width), width)

    def to_column(named, ssem, rsem):
        return [send(named, named, ssem.at[n], rsem.at[n], other) for n, (other, _) in enumerate(along_i)]

    def to_row(named, ssem, rsem):
        return [send(named, named, ssem.at[n], rsem.at[n], other) for n, (other, _) in enumerate(along_j)]

    def used_row(step_index):
        stars = (me_j * num_i + me_i) * width + lax.broadcasted_iota(jnp.int32, (width, lanes), 0)

        def match(row, seen):
            for inner in range(ids_all.shape[3]):
                names = ids_all[row // num_j, step_index, lax.rem(row, num_j), inner : inner + 1, :]
                seen = jnp.where(names == stars, 1.0, seen)
            return seen

        seen = lax.fori_loop(0, num_i * num_j, match, jnp.zeros((width, lanes), jnp.float32))
        column = jnp.broadcast_to(jnp.max(seen, axis=1, keepdims=True), (width, lanes))
        return jnp.transpose(column)[0:1] > 0.5

    def set_targets(rows):
        rows = jnp.concatenate([rows, jnp.zeros((lanes - 8, width), jnp.float32)], axis=0)
        columns = jnp.transpose(rows)
        for row in range(6):
            target_ref[row] = jnp.broadcast_to(columns[:, row : row + 1], (width, lanes))
        total_ref[...] = jnp.zeros_like(total_ref)

    def accumulate(source, owner):
        def tile(index, carry):
            rows = pl.ds(pl.multiple_of(index * TILE, TILE), TILE)
            tx, ty, tz, tu, tv, tw = [target_ref[row, rows, :] for row in range(6)]

            def chunk(block, sums):
                for first in range(0, width, lanes):
                    sx, sy, sz, su, sv, sw, mass = [
                        source[owner, block, row : row + 1, first : first + lanes] for row in range(7)
                    ]
                    ax, ay, az, jx, jy, jz = sums
                    dx, dy, dz = sx - tx, sy - ty, sz - tz
                    wx, wy, wz = su - tu, sv - tv, sw - tw
                    inverse = lax.rsqrt((dx * dx + dy * dy + dz * dz) + EPS2)
                    square = inverse * inverse
                    weight = (mass * inverse) * square
                    radial = (dx * wx + dy * wy + dz * wz) * (3.0 * square)
                    sums = (
                        ax + weight * dx,
                        ay + weight * dy,
                        az + weight * dz,
                        jx + weight * (wx - radial * dx),
                        jy + weight * (wy - radial * dy),
                        jz + weight * (wz - radial * dz),
                    )
                return sums

            sums = lax.fori_loop(0, num_i, chunk, tuple(total_ref[row, rows, :] for row in range(6)), unroll=True)
            for row in range(6):
                total_ref[row, rows, :] = sums[row]
            return carry

        lax.fori_loop(0, width // TILE, tile, 0)

    def totals():
        lane = lax.broadcasted_iota(jnp.int32, (width, lanes), 1)
        packed = jnp.zeros((width, lanes), jnp.float32)
        for row in range(6):
            packed = jnp.where(lane == row, jnp.sum(total_ref[row], axis=1, keepdims=True), packed)
        return jnp.transpose(packed)[0:6]

    def share(step_index, blocks):
        star = me_j * (num_i * width) + lax.broadcasted_iota(jnp.int32, (num_i * width, lanes), 0)
        table = pieces(jnp.concatenate(blocks, axis=1))
        tall = jnp.concatenate(table, axis=0)

        def fill(owner, carry):
            for row in range(ids_all.shape[3]):
                names = ids_all[me_i, step_index, owner, row : row + 1, :]
                onehot = jnp.where(star == names, 1.0, 0.0).astype(jnp.bfloat16)
                found = jnp.dot(tall, onehot, preferred_element_type=jnp.float32)
                part[step_index, owner, :, row * lanes : (row + 1) * lanes] = found[0:8] + found[8:16] + found[16:24]
            return carry

        lax.fori_loop(0, num_j, fill, 0)

    def send_parts(step_index, ssem, rsem):
        return [
            send(part.at[step_index, other[1]], got.at[step_index, me_j], ssem.at[n], rsem.at[n], other)
            for n, (other, _) in enumerate(along_j)
        ]

    loads = [
        pltpu.make_async_copy(source, target, load_sem.at[n])
        for n, (source, target) in enumerate((
            (counts_in, counts_ref), (raw_in, raw_ref), (level_in, level_ref), (mass_in, mass_ref), (state_in, state_ref)
        ))
    ]
    for copy in loads:
        copy.start()
    greeting = [other for other, _ in along_j + along_i]
    barrier = pltpu.get_barrier_semaphore()
    for other in greeting:
        pl.semaphore_signal(barrier, inc=1, device_id=other, device_id_type=MESH)
    for copy in loads:
        copy.wait()
    per_owner = ids_all.shape[3]
    slot = lax.broadcasted_iota(jnp.int32, (1, lanes), 1)
    for step_index in range(STEPS):
        for row in range(raw_ref.shape[1]):
            names = jnp.where(slot < counts_ref[step_index, row], raw_ref[step_index, row : row + 1, :], -1)
            inner = row % per_owner
            ids_all[me_i, step_index, row // per_owner, inner : inner + 1, :] = names
    mass_all = mass_ref[...]
    pos, vel = predict(state_ref[...], STEP_TIME + STEP_TIME * level_ref[...].astype(jnp.float32))
    for block in range(num_i):
        some = slice(block * width, (block + 1) * width)
        field[me_j, block] = jnp.concatenate([pos[:, some], vel[:, some], mass_all[:, some], mass_all[:, some]], axis=0)
    pl.semaphore_wait(barrier, len(greeting))
    loose = to_column(ids_all.at[me_i], sk, rk)
    coming = to_row(field.at[me_j], sf, rf)
    set_targets(field[me_j, me_i])
    accumulate(field, me_j)
    for copy in loose:
        copy.wait()
    used = used_row(0)
    for copy, (_, owner) in zip(coming, along_j):
        copy.wait_recv()
        accumulate(field, owner)
    for copy in coming:
        copy.wait_send()
    force = totals()
    state = state_ref[:, own]
    last = -STEP_TIME * level_ref[:, own].astype(jnp.float32)
    state = jnp.where(used, correct(state, force[0:3], force[3:6], STEP_TIME - last), state)
    last = jnp.where(used, STEP_TIME, last)
    span = 2 * STEP_TIME - last
    pos, vel = predict(state, span)
    mass = mass_ref[:, own]
    field_next[me_j, me_i] = jnp.concatenate([pos, vel, mass, mass], axis=0)
    blank = jnp.zeros((2, width), jnp.float32)
    rows_a[me_i] = jnp.concatenate([force, blank], axis=0)
    column = to_column(field_next.at[me_j, me_i], sa, ra)
    column_force = to_column(rows_a.at[me_i], sp, rp)
    set_targets(field_next[me_j, me_i])
    used = used_row(1)
    for copy in column:
        copy.wait()
    coming = to_row(field_next.at[me_j], sg, rg)
    accumulate(field_next, me_j)
    for copy in column_force:
        copy.wait()
    for copy, (_, owner) in zip(coming, along_j):
        copy.wait_recv()
        accumulate(field_next, owner)
    for copy in coming:
        copy.wait_send()
    force = totals()
    state = jnp.where(used, correct(state, force[0:3], force[3:6], span), state)
    rows_b[me_i] = jnp.concatenate([force, blank[:, :], state, blank, blank], axis=0)
    column = to_column(rows_b.at[me_i], sb, rb)
    share(0, [rows_a[block] for block in range(num_i)])
    first_parts = send_parts(0, sq.at[0], rq.at[0])
    for copy in column:
        copy.wait()
    share(1, [rows_b[block, 0:8, :] for block in range(num_i)])
    second_parts = send_parts(1, sq.at[1], rq.at[1])
    for block in range(num_i):
        out_ref[:, block * width : (block + 1) * width] = rows_b[block, 8:20, :]
    for step_index, parts in enumerate((first_parts, second_parts)):
        for copy in parts:
            copy.wait()
        total = part[step_index, me_j]
        for _, owner in along_j:
            total = total + got[step_index, owner]
        force_ref[step_index] = total[0:6]


def star_order(sizes, phase_space, star_mass, star_level, active_ids, active_counts):
    num_i, num_j = sizes
    shard = phase_space.shape[1]
    width = shard // num_i
    f32 = jnp.float32
    rows, lanes = active_ids.shape[1], active_ids.shape[2]
    share = (rows // num_j) * lanes
    dma_j, dma_i = pltpu.SemaphoreType.DMA((num_j - 1,)), pltpu.SemaphoreType.DMA((num_i - 1,))
    dma_2 = pltpu.SemaphoreType.DMA((STEPS, num_j - 1))
    return pl.pallas_call(
        functools.partial(whole_kernel, sizes),
        out_shape=(jax.ShapeDtypeStruct((12, shard), f32), jax.ShapeDtypeStruct((STEPS, 6, share), f32)),
        in_specs=[pl.BlockSpec(memory_space=pltpu.HBM)] * 5,
        out_specs=(VMEM,) * 2,
        scratch_shapes=[
            pltpu.VMEM((12, shard), f32),
            pltpu.VMEM((1, shard), f32),
            pltpu.VMEM((1, shard), jnp.int32),
            pltpu.VMEM(active_ids.shape, jnp.int32),
            pltpu.SMEM(active_counts.shape, jnp.int32),
            pltpu.VMEM((num_i, STEPS, num_j, rows // num_j, lanes), jnp.int32),
            pltpu.VMEM((num_j, num_i, 8, width), f32),
            pltpu.VMEM((num_j, num_i, 8, width), f32),
            pltpu.VMEM((num_i, 8, width), f32),
            pltpu.VMEM((num_i, 24, width), f32),
            pltpu.VMEM((STEPS, num_j, 8, share), f32),
            pltpu.VMEM((STEPS, num_j, 8, share), f32),
            pltpu.VMEM((6, width, 128), f32),
            pltpu.VMEM((6, width, 128), f32),
            pltpu.SemaphoreType.DMA((5,)), dma_i, dma_i, dma_j, dma_j, dma_j, dma_j, dma_i, dma_i, dma_i, dma_i, dma_i, dma_i, dma_2, dma_2,
        ],
        compiler_params=pltpu.CompilerParams(collective_id=0, has_side_effects=True, vmem_limit_bytes=63 * 2**20),
    )(phase_space, star_mass.reshape(1, shard), star_level.reshape(1, shard), active_ids, active_counts)


def solution(mesh):
    sizes = (mesh.shape["ia"], mesh.shape["ja"])
    placed = (P(None, "ja"), P("ja"), P("ja"), P(None, "ia", None), P(None, "ia"))

    def chosen(phase_space, star_mass, star_level, active_ids, active_counts):
        stars = phase_space.shape[1] * sizes[1]
        slots = active_ids.shape[1] * active_ids.shape[2] * sizes[0]
        if stars == slots:
            return star_order(sizes, phase_space, star_mass, star_level, active_ids, active_counts)
        return local(phase_space, star_mass, star_level, active_ids, active_counts)

    return jax.shard_map(
        chosen,
        mesh=mesh,
        in_specs=placed,
        out_specs=(P(None, "ja"), P(None, None, ("ia", "ja"))),
        check_vma=False,
    )
```

```python
import functools

import jax
import jax.numpy as jnp
from jax import lax
from jax.experimental import pallas as pl
from jax.experimental.pallas import tpu as pltpu
from jax.sharding import PartitionSpec as P

STEPS = 2


EPS2 = 0.01
STEP_TIME = 0.05


def predict(state, tau):
    tau_sq = tau * tau
    tau_cube = tau_sq * tau
    new_pos = (
        state[0:3] + state[3:6] * tau + state[6:9] * (tau_sq * 0.5) + state[9:12] * (tau_cube / 6.0)
    )
    new_vel = state[3:6] + state[6:9] * tau + state[9:12] * (tau_sq * 0.5)
    return (new_pos, new_vel)


def field_force(target_pos, target_vel, source_pos, source_vel, source_mass):
    offset = source_pos[:, None, :] - target_pos[:, :, None]
    rel_vel = source_vel[:, None, :] - target_vel[:, :, None]
    dist_sq = jnp.sum(offset * offset, axis=0) + EPS2
    inverse = lax.rsqrt(dist_sq)
    weight = source_mass[None, :] * inverse * inverse * inverse
    radial = 3.0 * jnp.sum(offset * rel_vel, axis=0) / dist_sq
    accel = jnp.sum(weight[None] * offset, axis=2)
    jolt = jnp.sum(weight[None] * (rel_vel - radial[None] * offset), axis=2)
    return jnp.concatenate([accel, jolt], axis=0)


def blocked_force(target_pos, target_vel, source_pos, source_vel, source_mass, block_rows):
    total_rows = target_pos.shape[1]
    block_count = total_rows // block_rows
    tiles = (
        target_pos.reshape(3, block_count, block_rows).transpose(1, 0, 2),
        target_vel.reshape(3, block_count, block_rows).transpose(1, 0, 2),
    )

    def one_tile(pair_tile):
        return field_force(pair_tile[0], pair_tile[1], source_pos, source_vel, source_mass)

    result = lax.map(one_tile, tiles)
    return result.transpose(1, 0, 2).reshape(6, total_rows)


def correct(active_rows, accel, jolt, span):
    half_step = span * 0.5
    twelfth = span * span / 12.0
    old_pos = active_rows[0:3]
    old_vel = active_rows[3:6]
    old_acc = active_rows[6:9]
    old_jerk = active_rows[9:12]
    new_vel = old_vel + (old_acc + accel) * half_step + (old_jerk - jolt) * twelfth
    new_pos = old_pos + (old_vel + new_vel) * half_step + (old_acc - accel) * twelfth
    return jnp.concatenate([new_pos, new_vel, accel, jolt], axis=0)


def local(phase_space, star_mass, star_level, active_ids, active_counts):
    shard_width = phase_space.shape[1]
    shard_start = lax.axis_index("ja") * shard_width
    block_rows = 512
    state = phase_space
    last = -STEP_TIME * star_level.astype(jnp.float32)
    force_steps = []
    for step_index in range(STEPS):
        clock = STEP_TIME * (step_index + 1)
        indices = active_ids[step_index].reshape(-1)
        slot_pos = lax.broadcasted_iota(jnp.int32, (active_ids.shape[1], active_ids.shape[2]), 1)
        usable = (slot_pos < active_counts[step_index][:, None]).reshape(-1)
        local_ids = indices - shard_start
        inside = (local_ids >= 0) & (local_ids < shard_width)
        clipped = jnp.clip(local_ids, 0, shard_width - 1)
        fpos, fvel = predict(state, clock - last)
        stacked = jnp.concatenate([state, last[None, :]], axis=0)
        picked = jnp.where(inside[None, :], jnp.take(stacked, clipped, axis=1), 0.0)
        target_state = lax.psum(picked, "ja")
        tpos, tvel = predict(target_state[0:12], clock - target_state[12])
        partial_value = blocked_force(tpos, tvel, fpos, fvel, star_mass, block_rows)
        write_ids = jnp.where(usable, indices, -1)
        forces = lax.psum(partial_value, "ja")
        share_len = forces.shape[1] // lax.axis_size("ja")
        share_start = lax.axis_index("ja") * share_len
        force_share = lax.dynamic_slice_in_dim(forces, share_start, share_len, 1)
        usable_share = lax.dynamic_slice_in_dim(usable, share_start, share_len, 0)
        force_steps.append(jnp.where(usable_share[None, :], force_share, 0.0))
        outgoing = correct(target_state[0:12], forces[0:3], forces[3:6], clock - target_state[12])
        returned, return_ids = (
            lax.all_gather(outgoing, "ia", axis=1, tiled=True),
            lax.all_gather(write_ids, "ia", axis=0, tiled=True),
        )
        placed_raw = return_ids - shard_start
        valid = (return_ids >= 0) & (placed_raw >= 0) & (placed_raw < shard_width)
        placed = jnp.where(valid, placed_raw, shard_width)
        state = state.at[:, placed].set(returned, mode="drop")
        last = last.at[placed].set(clock, mode="drop")
    return (state, jnp.stack(force_steps))


MESH = pl.DeviceIdType.MESH
TILE = 16
VMEM = pl.BlockSpec(memory_space=pltpu.VMEM)


def pieces(values):
    high = values.astype(jnp.bfloat16)
    rest = values - high.astype(jnp.float32)
    middle = rest.astype(jnp.bfloat16)
    low = (rest - middle.astype(jnp.float32)).astype(jnp.bfloat16)
    return high, middle, low


def peers(sizes):
    num_i, num_j = sizes
    me_i, me_j = lax.axis_index("ia"), lax.axis_index("ja")
    chips, chip, core = num_j // 2, me_j // 2, lax.rem(me_j, 2)
    steps = sorted(range(chips), key=lambda step: min(step, chips - step))
    along_j = []
    for step in steps:
        for flip in (0, 1):
            if step or flip:
                side = lax.rem(core + flip, 2)
                ahead = lax.rem(chip + step, chips) * 2 + side
                behind = lax.rem(chip + chips - step, chips) * 2 + side
                along_j.append(((me_i, ahead), behind))
    along_i = [((lax.rem(me_i + step, num_i), me_j), lax.rem(me_i + num_i - step, num_i)) for step in range(1, num_i)]
    return along_j, along_i


def send(source, target, send_sem, recv_sem, other):
    copy = pltpu.make_async_remote_copy(
        src_ref=source,
        dst_ref=target,
        send_sem=send_sem,
        recv_sem=recv_sem,
        device_id=other,
        device_id_type=MESH,
    )
    copy.start()
    return copy


def whole_kernel(
    sizes, state_in, mass_in, level_in, raw_in, counts_in, out_ref, force_ref,
    state_ref, mass_ref, level_ref, raw_ref, counts_ref, ids_all, field, field_next, rows_a, rows_b, part, got, target_ref, total_ref,
    load_sem, sk, rk, sf, rf, sg, rg, sa, ra, sb, rb, sp, rp, sq, rq,
):
    num_i, num_j = sizes
    me_i, me_j = lax.axis_index("ia"), lax.axis_index("ja")
    width, lanes = rows_a.shape[2], 128
    along_j, along_i = peers(sizes)
    own = pl.ds(pl.multiple_of(me_i * width, width), width)

    def to_column(named, ssem, rsem):
        return [send(named, named, ssem.at[n], rsem.at[n], other) for n, (other, _) in enumerate(along_i)]

    def to_row(named, ssem, rsem):
        return [send(named, named, ssem.at[n], rsem.at[n], other) for n, (other, _) in enumerate(along_j)]

    def used_row(step_index):
        stars = (me_j * num_i + me_i) * width + lax.broadcasted_iota(jnp.int32, (width, lanes), 0)

        def match(row, seen):
            for inner in range(ids_all.shape[3]):
                names = ids_all[row // num_j, step_index, lax.rem(row, num_j), inner : inner + 1, :]
                seen = jnp.where(names == stars, 1.0, seen)
            return seen

        seen = lax.fori_loop(0, num_i * num_j, match, jnp.zeros((width, lanes), jnp.float32))
        column = jnp.broadcast_to(jnp.max(seen, axis=1, keepdims=True), (width, lanes))
        return jnp.transpose(column)[0:1] > 0.5

    def set_targets(rows):
        rows = jnp.concatenate([rows, jnp.zeros((lanes - 8, width), jnp.float32)], axis=0)
        columns = jnp.transpose(rows)
        for row in range(6):
            target_ref[row] = jnp.broadcast_to(columns[:, row : row + 1], (width, lanes))
        total_ref[...] = jnp.zeros_like(total_ref)

    def accumulate(source, owner):
        def tile(index, carry):
            rows = pl.ds(pl.multiple_of(index * TILE, TILE), TILE)
            tx, ty, tz, tu, tv, tw = [target_ref[row, rows, :] for row in range(6)]

            def chunk(block, sums):
                for first in range(0, width, lanes):
                    sx, sy, sz, su, sv, sw, mass = [
                        source[owner, block, row : row + 1, first : first + lanes] for row in range(7)
                    ]
                    ax, ay, az, jx, jy, jz = sums
                    dx, dy, dz = sx - tx, sy - ty, sz - tz
                    wx, wy, wz = su - tu, sv - tv, sw - tw
                    inverse = lax.rsqrt((dx * dx + dy * dy + dz * dz) + EPS2)
                    square = inverse * inverse
                    weight = (mass * inverse) * square
                    radial = (dx * wx + dy * wy + dz * wz) * (3.0 * square)
                    sums = (
                        ax + weight * dx,
                        ay + weight * dy,
                        az + weight * dz,
                        jx + weight * (wx - radial * dx),
                        jy + weight * (wy - radial * dy),
                        jz + weight * (wz - radial * dz),
                    )
                return sums

            sums = lax.fori_loop(0, num_i, chunk, tuple(total_ref[row, rows, :] for row in range(6)), unroll=True)
            for row in range(6):
                total_ref[row, rows, :] = sums[row]
            return carry

        lax.fori_loop(0, width // TILE, tile, 0)

    def totals():
        lane = lax.broadcasted_iota(jnp.int32, (width, lanes), 1)
        packed = jnp.zeros((width, lanes), jnp.float32)
        for row in range(6):
            packed = jnp.where(lane == row, jnp.sum(total_ref[row], axis=1, keepdims=True), packed)
        return jnp.transpose(packed)[0:6]

    def share(step_index, blocks):
        star = me_j * (num_i * width) + lax.broadcasted_iota(jnp.int32, (num_i * width, lanes), 0)
        table = pieces(jnp.concatenate(blocks, axis=1))
        tall = jnp.concatenate(table, axis=0)

        def fill(owner, carry):
            for row in range(ids_all.shape[3]):
                names = ids_all[me_i, step_index, owner, row : row + 1, :]
                onehot = jnp.where(star == names, 1.0, 0.0).astype(jnp.bfloat16)
                found = jnp.dot(tall, onehot, preferred_element_type=jnp.float32)
                part[step_index, owner, :, row * lanes : (row + 1) * lanes] = found[0:8] + found[8:16] + found[16:24]
            return carry

        lax.fori_loop(0, num_j, fill, 0)

    def send_parts(step_index, ssem, rsem):
        return [
            send(part.at[step_index, other[1]], got.at[step_index, me_j], ssem.at[n], rsem.at[n], other)
            for n, (other, _) in enumerate(along_j)
        ]

    loads = [
        pltpu.make_async_copy(source, target, load_sem.at[n])
        for n, (source, target) in enumerate((
            (counts_in, counts_ref), (raw_in, raw_ref), (level_in, level_ref), (mass_in, mass_ref), (state_in, state_ref)
        ))
    ]
    for copy in loads:
        copy.start()
    greeting = [other for other, _ in along_j + along_i]
    barrier = pltpu.get_barrier_semaphore()
    for other in greeting:
        pl.semaphore_signal(barrier, inc=1, device_id=other, device_id_type=MESH)
    for copy in loads:
        copy.wait()
    per_owner = ids_all.shape[3]
    slot = lax.broadcasted_iota(jnp.int32, (1, lanes), 1)
    for step_index in range(STEPS):
        for row in range(raw_ref.shape[1]):
            names = jnp.where(slot < counts_ref[step_index, row], raw_ref[step_index, row : row + 1, :], -1)
            inner = row % per_owner
            ids_all[me_i, step_index, row // per_owner, inner : inner + 1, :] = names
    mass_all = mass_ref[...]
    pos, vel = predict(state_ref[...], STEP_TIME + STEP_TIME * level_ref[...].astype(jnp.float32))
    for block in range(num_i):
        some = slice(block * width, (block + 1) * width)
        field[me_j, block] = jnp.concatenate([pos[:, some], vel[:, some], mass_all[:, some], mass_all[:, some]], axis=0)
    pl.semaphore_wait(barrier, len(greeting))
    loose = to_column(ids_all.at[me_i], sk, rk)
    coming = to_row(field.at[me_j], sf, rf)
    set_targets(field[me_j, me_i])
    accumulate(field, me_j)
    for copy in loose:
        copy.wait()
    used = used_row(0)
    for copy, (_, owner) in zip(coming, along_j):
        copy.wait_recv()
        accumulate(field, owner)
    for copy in coming:
        copy.wait_send()
    force = totals()
    state = state_ref[:, own]
    last = -STEP_TIME * level_ref[:, own].astype(jnp.float32)
    state = jnp.where(used, correct(state, force[0:3], force[3:6], STEP_TIME - last), state)
    last = jnp.where(used, STEP_TIME, last)
    span = 2 * STEP_TIME - last
    pos, vel = predict(state, span)
    mass = mass_ref[:, own]
    field_next[me_j, me_i] = jnp.concatenate([pos, vel, mass, mass], axis=0)
    blank = jnp.zeros((2, width), jnp.float32)
    rows_a[me_i] = jnp.concatenate([force, blank], axis=0)
    column = to_column(field_next.at[me_j, me_i], sa, ra)
    column_force = to_column(rows_a.at[me_i], sp, rp)
    set_targets(field_next[me_j, me_i])
    used = used_row(1)
    for copy in column:
        copy.wait()
    coming = to_row(field_next.at[me_j], sg, rg)
    accumulate(field_next, me_j)
    for copy in column_force:
        copy.wait()
    for copy, (_, owner) in zip(coming, along_j):
        copy.wait_recv()
        accumulate(field_next, owner)
    for copy in coming:
        copy.wait_send()
    force = totals()
    state = jnp.where(used, correct(state, force[0:3], force[3:6], span), state)
    rows_b[me_i] = jnp.concatenate([force, blank[:, :], state, blank, blank], axis=0)
    column = to_column(rows_b.at[me_i], sb, rb)
    share(0, [rows_a[block] for block in range(num_i)])
    first_parts = send_parts(0, sq.at[0], rq.at[0])
    for copy in column:
        copy.wait()
    share(1, [rows_b[block, 0:8, :] for block in range(num_i)])
    second_parts = send_parts(1, sq.at[1], rq.at[1])
    for block in range(num_i):
        out_ref[:, block * width : (block + 1) * width] = rows_b[block, 8:20, :]
    for step_index, parts in enumerate((first_parts, second_parts)):
        for copy in parts:
            copy.wait()
        total = part[step_index, me_j]
        for _, owner in along_j:
            total = total + got[step_index, owner]
        force_ref[step_index] = total[0:6]


def star_order(sizes, phase_space, star_mass, star_level, active_ids, active_counts):
    num_i, num_j = sizes
    shard = phase_space.shape[1]
    width = shard // num_i
    f32 = jnp.float32
    rows, lanes = active_ids.shape[1], active_ids.shape[2]
    share = (rows // num_j) * lanes
    operands = (phase_space, star_mass.reshape(1, shard), star_level.reshape(1, shard), active_ids, active_counts)
    dma_j, dma_i = pltpu.SemaphoreType.DMA((num_j - 1,)), pltpu.SemaphoreType.DMA((num_i - 1,))
    dma_2 = pltpu.SemaphoreType.DMA((STEPS, num_j - 1))
    return pl.pallas_call(
        functools.partial(whole_kernel, sizes),
        out_shape=(jax.ShapeDtypeStruct((12, shard), f32), jax.ShapeDtypeStruct((STEPS, 6, share), f32)),
        in_specs=[pl.BlockSpec(memory_space=pltpu.HBM)] * 5,
        out_specs=(VMEM,) * 2,
        scratch_shapes=[
            pltpu.VMEM((12, shard), f32),
            pltpu.VMEM((1, shard), f32),
            pltpu.VMEM((1, shard), jnp.int32),
            pltpu.VMEM(active_ids.shape, jnp.int32),
            pltpu.SMEM(active_counts.shape, jnp.int32),
            pltpu.VMEM((num_i, STEPS, num_j, rows // num_j, lanes), jnp.int32),
            pltpu.VMEM((num_j, num_i, 8, width), f32),
            pltpu.VMEM((num_j, num_i, 8, width), f32),
            pltpu.VMEM((num_i, 8, width), f32),
            pltpu.VMEM((num_i, 24, width), f32),
            pltpu.VMEM((STEPS, num_j, 8, share), f32),
            pltpu.VMEM((STEPS, num_j, 8, share), f32),
            pltpu.VMEM((6, width, 128), f32),
            pltpu.VMEM((6, width, 128), f32),
            pltpu.SemaphoreType.DMA((5,)), dma_i, dma_i, dma_j, dma_j, dma_j, dma_j, dma_i, dma_i, dma_i, dma_i, dma_i, dma_i, dma_2, dma_2,
        ],
        compiler_params=pltpu.CompilerParams(collective_id=0, has_side_effects=True, vmem_limit_bytes=32 * 2**20),
    )(*[pltpu.with_memory_space_constraint(array, pltpu.HBM) for array in operands])


def solution(mesh):
    sizes = (mesh.shape["ia"], mesh.shape["ja"])
    placed = (P(None, "ja"), P("ja"), P("ja"), P(None, "ia", None), P(None, "ia"))

    def chosen(phase_space, star_mass, star_level, active_ids, active_counts):
        stars = phase_space.shape[1] * sizes[1]
        slots = active_ids.shape[1] * active_ids.shape[2] * sizes[0]
        if stars == slots:
            return star_order(sizes, phase_space, star_mass, star_level, active_ids, active_counts)
        return local(phase_space, star_mass, star_level, active_ids, active_counts)

    return jax.shard_map(
        chosen,
        mesh=mesh,
        in_specs=placed,
        out_specs=(P(None, "ja"), P(None, None, ("ia", "ja"))),
        check_vma=False,
    )
```

```python
import functools

import jax
import jax.numpy as jnp
from jax import lax
from jax.experimental import pallas as pl
from jax.experimental.pallas import tpu as pltpu
from jax.sharding import PartitionSpec as P

STEPS = 2


EPS2 = 0.01
STEP_TIME = 0.05


def predict(state, tau):
    tau_sq = tau * tau
    tau_cube = tau_sq * tau
    new_pos = (
        state[0:3] + state[3:6] * tau + state[6:9] * (tau_sq * 0.5) + state[9:12] * (tau_cube / 6.0)
    )
    new_vel = state[3:6] + state[6:9] * tau + state[9:12] * (tau_sq * 0.5)
    return (new_pos, new_vel)


def field_force(target_pos, target_vel, source_pos, source_vel, source_mass):
    offset = source_pos[:, None, :] - target_pos[:, :, None]
    rel_vel = source_vel[:, None, :] - target_vel[:, :, None]
    dist_sq = jnp.sum(offset * offset, axis=0) + EPS2
    inverse = lax.rsqrt(dist_sq)
    weight = source_mass[None, :] * inverse * inverse * inverse
    radial = 3.0 * jnp.sum(offset * rel_vel, axis=0) / dist_sq
    accel = jnp.sum(weight[None] * offset, axis=2)
    jolt = jnp.sum(weight[None] * (rel_vel - radial[None] * offset), axis=2)
    return jnp.concatenate([accel, jolt], axis=0)


def blocked_force(target_pos, target_vel, source_pos, source_vel, source_mass, block_rows):
    total_rows = target_pos.shape[1]
    block_count = total_rows // block_rows
    tiles = (
        target_pos.reshape(3, block_count, block_rows).transpose(1, 0, 2),
        target_vel.reshape(3, block_count, block_rows).transpose(1, 0, 2),
    )

    def one_tile(pair_tile):
        return field_force(pair_tile[0], pair_tile[1], source_pos, source_vel, source_mass)

    result = lax.map(one_tile, tiles)
    return result.transpose(1, 0, 2).reshape(6, total_rows)


def correct(active_rows, accel, jolt, span):
    half_step = span * 0.5
    twelfth = span * span / 12.0
    old_pos = active_rows[0:3]
    old_vel = active_rows[3:6]
    old_acc = active_rows[6:9]
    old_jerk = active_rows[9:12]
    new_vel = old_vel + (old_acc + accel) * half_step + (old_jerk - jolt) * twelfth
    new_pos = old_pos + (old_vel + new_vel) * half_step + (old_acc - accel) * twelfth
    return jnp.concatenate([new_pos, new_vel, accel, jolt], axis=0)


def local(phase_space, star_mass, star_level, active_ids, active_counts):
    shard_width = phase_space.shape[1]
    shard_start = lax.axis_index("ja") * shard_width
    block_rows = 512
    state = phase_space
    last = -STEP_TIME * star_level.astype(jnp.float32)
    force_steps = []
    for step_index in range(STEPS):
        clock = STEP_TIME * (step_index + 1)
        indices = active_ids[step_index].reshape(-1)
        slot_pos = lax.broadcasted_iota(jnp.int32, (active_ids.shape[1], active_ids.shape[2]), 1)
        usable = (slot_pos < active_counts[step_index][:, None]).reshape(-1)
        local_ids = indices - shard_start
        inside = (local_ids >= 0) & (local_ids < shard_width)
        clipped = jnp.clip(local_ids, 0, shard_width - 1)
        fpos, fvel = predict(state, clock - last)
        stacked = jnp.concatenate([state, last[None, :]], axis=0)
        picked = jnp.where(inside[None, :], jnp.take(stacked, clipped, axis=1), 0.0)
        target_state = lax.psum(picked, "ja")
        tpos, tvel = predict(target_state[0:12], clock - target_state[12])
        partial_value = blocked_force(tpos, tvel, fpos, fvel, star_mass, block_rows)
        write_ids = jnp.where(usable, indices, -1)
        forces = lax.psum(partial_value, "ja")
        share_len = forces.shape[1] // lax.axis_size("ja")
        share_start = lax.axis_index("ja") * share_len
        force_share = lax.dynamic_slice_in_dim(forces, share_start, share_len, 1)
        usable_share = lax.dynamic_slice_in_dim(usable, share_start, share_len, 0)
        force_steps.append(jnp.where(usable_share[None, :], force_share, 0.0))
        outgoing = correct(target_state[0:12], forces[0:3], forces[3:6], clock - target_state[12])
        returned, return_ids = (
            lax.all_gather(outgoing, "ia", axis=1, tiled=True),
            lax.all_gather(write_ids, "ia", axis=0, tiled=True),
        )
        placed_raw = return_ids - shard_start
        valid = (return_ids >= 0) & (placed_raw >= 0) & (placed_raw < shard_width)
        placed = jnp.where(valid, placed_raw, shard_width)
        state = state.at[:, placed].set(returned, mode="drop")
        last = last.at[placed].set(clock, mode="drop")
    return (state, jnp.stack(force_steps))


MESH = pl.DeviceIdType.MESH
TILE = 16
VMEM = pl.BlockSpec(memory_space=pltpu.VMEM)


def pieces(values):
    high = values.astype(jnp.bfloat16)
    rest = values - high.astype(jnp.float32)
    middle = rest.astype(jnp.bfloat16)
    low = (rest - middle.astype(jnp.float32)).astype(jnp.bfloat16)
    return high, middle, low


def peers(sizes):
    num_i, num_j = sizes
    me_i, me_j = lax.axis_index("ia"), lax.axis_index("ja")
    chips, chip, core = num_j // 2, me_j // 2, lax.rem(me_j, 2)
    steps = sorted(range(chips), key=lambda step: min(step, chips - step))
    along_j = []
    for step in steps:
        for flip in (0, 1):
            if step or flip:
                side = lax.rem(core + flip, 2)
                ahead = lax.rem(chip + step, chips) * 2 + side
                behind = lax.rem(chip + chips - step, chips) * 2 + side
                along_j.append(((me_i, ahead), behind))
    along_i = [((lax.rem(me_i + step, num_i), me_j), lax.rem(me_i + num_i - step, num_i)) for step in range(1, num_i)]
    return along_j, along_i


def send(source, target, send_sem, recv_sem, other):
    copy = pltpu.make_async_remote_copy(
        src_ref=source,
        dst_ref=target,
        send_sem=send_sem,
        recv_sem=recv_sem,
        device_id=other,
        device_id_type=MESH,
    )
    copy.start()
    return copy


def whole_kernel(
    sizes, state_in, mass_in, level_in, raw_in, counts_in, out_ref, force_ref,
    state_ref, mass_ref, level_ref, raw_ref, counts_ref, ids_all, field, field_next, rows_a, rows_b, part, got, target_ref, total_ref,
    load_sem, sk, rk, sf, rf, sg, rg, sa, ra, sb, rb, sp, rp, sq, rq,
):
    num_i, num_j = sizes
    me_i, me_j = lax.axis_index("ia"), lax.axis_index("ja")
    width, lanes = rows_a.shape[2], 128
    along_j, along_i = peers(sizes)
    own = pl.ds(pl.multiple_of(me_i * width, width), width)

    def to_column(named, ssem, rsem):
        return [send(named, named, ssem.at[n], rsem.at[n], other) for n, (other, _) in enumerate(along_i)]

    def to_row(named, ssem, rsem):
        return [send(named, named, ssem.at[n], rsem.at[n], other) for n, (other, _) in enumerate(along_j)]

    def used_row(step_index):
        stars = (me_j * num_i + me_i) * width + lax.broadcasted_iota(jnp.int32, (width, lanes), 0)

        def match(row, seen):
            for inner in range(ids_all.shape[3]):
                names = ids_all[row // num_j, step_index, lax.rem(row, num_j), inner : inner + 1, :]
                seen = jnp.where(names == stars, 1.0, seen)
            return seen

        seen = lax.fori_loop(0, num_i * num_j, match, jnp.zeros((width, lanes), jnp.float32))
        column = jnp.broadcast_to(jnp.max(seen, axis=1, keepdims=True), (width, lanes))
        return jnp.transpose(column)[0:1] > 0.5

    def set_targets(rows):
        rows = jnp.concatenate([rows, jnp.zeros((lanes - 8, width), jnp.float32)], axis=0)
        columns = jnp.transpose(rows)
        for row in range(6):
            target_ref[row] = jnp.broadcast_to(columns[:, row : row + 1], (width, lanes))
        total_ref[...] = jnp.zeros_like(total_ref)

    def accumulate(source, owner, start=0, stop=num_i, turn=0):
        def tile(index, carry):
            rows = pl.ds(pl.multiple_of(index * TILE, TILE), TILE)
            tx, ty, tz, tu, tv, tw = [target_ref[row, rows, :] for row in range(6)]

            def chunk(count, sums):
                block = lax.rem(count + turn, num_i)
                for first in range(0, width, lanes):
                    sx, sy, sz, su, sv, sw, mass = [
                        source[owner, block, row : row + 1, first : first + lanes] for row in range(7)
                    ]
                    ax, ay, az, jx, jy, jz = sums
                    dx, dy, dz = sx - tx, sy - ty, sz - tz
                    wx, wy, wz = su - tu, sv - tv, sw - tw
                    inverse = lax.rsqrt((dx * dx + dy * dy + dz * dz) + EPS2)
                    square = inverse * inverse
                    weight = (mass * inverse) * square
                    radial = (dx * wx + dy * wy + dz * wz) * (3.0 * square)
                    sums = (
                        ax + weight * dx,
                        ay + weight * dy,
                        az + weight * dz,
                        jx + weight * (wx - radial * dx),
                        jy + weight * (wy - radial * dy),
                        jz + weight * (wz - radial * dz),
                    )
                return sums

            sums = lax.fori_loop(start, stop, chunk, tuple(total_ref[row, rows, :] for row in range(6)), unroll=True)
            for row in range(6):
                total_ref[row, rows, :] = sums[row]
            return carry

        lax.fori_loop(0, width // TILE, tile, 0)

    def totals():
        lane = lax.broadcasted_iota(jnp.int32, (width, lanes), 1)
        packed = jnp.zeros((width, lanes), jnp.float32)
        for row in range(6):
            packed = jnp.where(lane == row, jnp.sum(total_ref[row], axis=1, keepdims=True), packed)
        return jnp.transpose(packed)[0:6]

    def share(step_index, blocks):
        star = me_j * (num_i * width) + lax.broadcasted_iota(jnp.int32, (num_i * width, lanes), 0)
        table = pieces(jnp.concatenate(blocks, axis=1))
        tall = jnp.concatenate(table, axis=0)

        def fill(owner, carry):
            for row in range(ids_all.shape[3]):
                names = ids_all[me_i, step_index, owner, row : row + 1, :]
                onehot = jnp.where(star == names, 1.0, 0.0).astype(jnp.bfloat16)
                found = jnp.dot(tall, onehot, preferred_element_type=jnp.float32)
                part[step_index, owner, :, row * lanes : (row + 1) * lanes] = found[0:8] + found[8:16] + found[16:24]
            return carry

        lax.fori_loop(0, num_j, fill, 0)

    def send_parts(step_index, ssem, rsem):
        return [
            send(part.at[step_index, other[1]], got.at[step_index, me_j], ssem.at[n], rsem.at[n], other)
            for n, (other, _) in enumerate(along_j)
        ]

    loads = [
        pltpu.make_async_copy(source, target, load_sem.at[n])
        for n, (source, target) in enumerate((
            (counts_in, counts_ref), (raw_in, raw_ref), (level_in, level_ref), (mass_in, mass_ref), (state_in, state_ref)
        ))
    ]
    for copy in loads:
        copy.start()
    greeting = [other for other, _ in along_j + along_i]
    barrier = pltpu.get_barrier_semaphore()
    for other in greeting:
        pl.semaphore_signal(barrier, inc=1, device_id=other, device_id_type=MESH)
    for copy in loads:
        copy.wait()
    per_owner = ids_all.shape[3]
    slot = lax.broadcasted_iota(jnp.int32, (1, lanes), 1)
    for step_index in range(STEPS):
        for row in range(raw_ref.shape[1]):
            names = jnp.where(slot < counts_ref[step_index, row], raw_ref[step_index, row : row + 1, :], -1)
            inner = row % per_owner
            ids_all[me_i, step_index, row // per_owner, inner : inner + 1, :] = names
    mass_all = mass_ref[...]
    pos, vel = predict(state_ref[...], STEP_TIME + STEP_TIME * level_ref[...].astype(jnp.float32))
    for block in range(num_i):
        some = slice(block * width, (block + 1) * width)
        field[me_j, block] = jnp.concatenate([pos[:, some], vel[:, some], mass_all[:, some], mass_all[:, some]], axis=0)
    pl.semaphore_wait(barrier, len(greeting))
    loose = to_column(ids_all.at[me_i], sk, rk)
    coming = to_row(field.at[me_j], sf, rf)
    set_targets(field[me_j, me_i])
    accumulate(field, me_j)
    for copy in loose:
        copy.wait()
    used = used_row(0)
    for copy, (_, owner) in zip(coming, along_j):
        copy.wait_recv()
        accumulate(field, owner)
    for copy in coming:
        copy.wait_send()
    force = totals()
    state = state_ref[:, own]
    last = -STEP_TIME * level_ref[:, own].astype(jnp.float32)
    state = jnp.where(used, correct(state, force[0:3], force[3:6], STEP_TIME - last), state)
    last = jnp.where(used, STEP_TIME, last)
    span = 2 * STEP_TIME - last
    pos, vel = predict(state, span)
    mass = mass_ref[:, own]
    field_next[me_j, me_i] = jnp.concatenate([pos, vel, mass, mass], axis=0)
    blank = jnp.zeros((2, width), jnp.float32)
    rows_a[me_i] = jnp.concatenate([force, blank], axis=0)
    column = to_column(field_next.at[me_j, me_i], sa, ra)
    column_force = to_column(rows_a.at[me_i], sp, rp)
    set_targets(field_next[me_j, me_i])
    used = used_row(1)
    accumulate(field_next, me_j, 0, 1, me_i)
    for copy in column:
        copy.wait()
    coming = to_row(field_next.at[me_j], sg, rg)
    accumulate(field_next, me_j, 1, num_i, me_i)
    for copy in column_force:
        copy.wait()
    for copy, (_, owner) in zip(coming, along_j):
        copy.wait_recv()
        accumulate(field_next, owner)
    for copy in coming:
        copy.wait_send()
    force = totals()
    state = jnp.where(used, correct(state, force[0:3], force[3:6], span), state)
    rows_b[me_i] = jnp.concatenate([force, blank[:, :], state, blank, blank], axis=0)
    column = to_column(rows_b.at[me_i], sb, rb)
    share(0, [rows_a[block] for block in range(num_i)])
    first_parts = send_parts(0, sq.at[0], rq.at[0])
    for copy in column:
        copy.wait()
    share(1, [rows_b[block, 0:8, :] for block in range(num_i)])
    second_parts = send_parts(1, sq.at[1], rq.at[1])
    for block in range(num_i):
        out_ref[:, block * width : (block + 1) * width] = rows_b[block, 8:20, :]
    for step_index, parts in enumerate((first_parts, second_parts)):
        for copy in parts:
            copy.wait()
        total = part[step_index, me_j]
        for _, owner in along_j:
            total = total + got[step_index, owner]
        force_ref[step_index] = total[0:6]


def star_order(sizes, phase_space, star_mass, star_level, active_ids, active_counts):
    num_i, num_j = sizes
    shard = phase_space.shape[1]
    width = shard // num_i
    f32 = jnp.float32
    rows, lanes = active_ids.shape[1], active_ids.shape[2]
    share = (rows // num_j) * lanes
    operands = (phase_space, star_mass.reshape(1, shard), star_level.reshape(1, shard), active_ids, active_counts)
    dma_j, dma_i = pltpu.SemaphoreType.DMA((num_j - 1,)), pltpu.SemaphoreType.DMA((num_i - 1,))
    dma_2 = pltpu.SemaphoreType.DMA((STEPS, num_j - 1))
    return pl.pallas_call(
        functools.partial(whole_kernel, sizes),
        out_shape=(jax.ShapeDtypeStruct((12, shard), f32), jax.ShapeDtypeStruct((STEPS, 6, share), f32)),
        in_specs=[pl.BlockSpec(memory_space=pltpu.HBM)] * 5,
        out_specs=(VMEM,) * 2,
        scratch_shapes=[
            pltpu.VMEM((12, shard), f32),
            pltpu.VMEM((1, shard), f32),
            pltpu.VMEM((1, shard), jnp.int32),
            pltpu.VMEM(active_ids.shape, jnp.int32),
            pltpu.SMEM(active_counts.shape, jnp.int32),
            pltpu.VMEM((num_i, STEPS, num_j, rows // num_j, lanes), jnp.int32),
            pltpu.VMEM((num_j, num_i, 8, width), f32),
            pltpu.VMEM((num_j, num_i, 8, width), f32),
            pltpu.VMEM((num_i, 8, width), f32),
            pltpu.VMEM((num_i, 24, width), f32),
            pltpu.VMEM((STEPS, num_j, 8, share), f32),
            pltpu.VMEM((STEPS, num_j, 8, share), f32),
            pltpu.VMEM((6, width, 128), f32),
            pltpu.VMEM((6, width, 128), f32),
            pltpu.SemaphoreType.DMA((5,)), dma_i, dma_i, dma_j, dma_j, dma_j, dma_j, dma_i, dma_i, dma_i, dma_i, dma_i, dma_i, dma_2, dma_2,
        ],
        compiler_params=pltpu.CompilerParams(collective_id=0, has_side_effects=True, vmem_limit_bytes=32 * 2**20),
    )(*[pltpu.with_memory_space_constraint(array, pltpu.HBM) for array in operands])


def solution(mesh):
    sizes = (mesh.shape["ia"], mesh.shape["ja"])
    placed = (P(None, "ja"), P("ja"), P("ja"), P(None, "ia", None), P(None, "ia"))

    def chosen(phase_space, star_mass, star_level, active_ids, active_counts):
        stars = phase_space.shape[1] * sizes[1]
        slots = active_ids.shape[1] * active_ids.shape[2] * sizes[0]
        if stars == slots:
            return star_order(sizes, phase_space, star_mass, star_level, active_ids, active_counts)
        return local(phase_space, star_mass, star_level, active_ids, active_counts)

    return jax.shard_map(
        chosen,
        mesh=mesh,
        in_specs=placed,
        out_specs=(P(None, "ja"), P(None, None, ("ia", "ja"))),
        check_vma=False,
    )
```
